256 devices in a mesh: noise: 32 (over z, y), dp: 8 (over x, core).
Axes of the slice: x: 4, y: 4, z: 8, core: 2. Of those that a mesh axis runs over, the one named last changes fastest.
Arguments:
- noise_batch: bfloat16 [32768, 1024], P('noise', 'dp'), may hold values from -6 to 6
- latents: bfloat16 [16384, 1024], P('dp', 'noise'), may hold values from -6 to 6
Outputs:
- row_potential: float32 [32768], P('noise')
- col_potential: float32 [16384], P('dp')
- target: bfloat16 [32768, 1024], P('noise', 'dp')
The draws below stay inside these ranges and needn't reach their ends.
All inputs are finite; a program needn't handle non-finite values.
Results may differ from the reference program's by a relative error of at most 0.015.
Values may be sent and summed in bfloat16 or wider, within the bound.
A program may use at most 64 MiB of HBM per device.

```python
import math
import jax
import jax.numpy as jnp

D = 1024
COLS_DEV = 2048
ITERS = 3
NN = 32768
NM = 16384
N_DP = 8


def levels(key, dims, shards, smallest, top_value):
    def one(dim, shards_of):
        draws = jax.random.uniform(jax.random.fold_in(jax.random.fold_in(key, 6), dim), (shards_of,), jnp.float32, smallest / len(shards), top_value / len(shards))
        return jnp.repeat(jnp.exp(draws), dims[dim] // shards_of).reshape((-1,) + (1,) * (len(dims) - dim - 1))

    gain = one(*shards[0])
    for cut in shards[1:]:
        gain = gain * one(*cut)
    return gain


def bell_draw(own_key, extent, scale, bound, split=(), held_as=jnp.bfloat16):
    values = scale * jax.random.normal(own_key, extent, jnp.float32)
    if split:
        values = values * levels(own_key, extent, split, -0.22, 0.18)
    return jnp.clip(values, -bound, bound).astype(held_as)


def setup_inputs(seed: int = 0) -> dict:
    key_of = jax.random.split(jax.random.key(seed), 3)
    noise_batch = bell_draw(key_of[0], (NN, D), 1.0, 6.0, ((0, 32), (1, 8)))
    latents = bell_draw(key_of[1], (NM, D), 1.0, 6.0, ((0, 8), (1, 32)))
    return dict(noise_batch=noise_batch, latents=latents)


epsilon = 0.01


def build_cost(noise_batch, latents):
    noise_f = noise_batch.astype(jnp.float32)
    latent_f = latents.astype(jnp.float32)
    row_norms = jnp.sum(noise_f * noise_f, axis=1)
    col_norms = jnp.sum(latent_f * latent_f, axis=1)
    cross_term = jnp.dot(noise_batch, latents.T, preferred_element_type=jnp.float32)
    return (row_norms[:, None] + col_norms[None, :] - 2.0 * cross_term) / D


def log_sum_exp(scaled, axis_pick):
    peak_value = jnp.max(scaled, axis=axis_pick, keepdims=True)
    exp_total = jnp.sum(jnp.exp(scaled - peak_value), axis=axis_pick)
    return jnp.squeeze(peak_value, axis=axis_pick) + jnp.log(exp_total)


def reference(noise_batch, latents):
    cost_tile = build_cost(noise_batch, latents)
    row_potential = jnp.zeros((NN,), jnp.float32)
    col_potential = jnp.zeros((NM,), jnp.float32)
    for step in range(ITERS):
        col_potential = -epsilon * math.log(NM) - epsilon * log_sum_exp((row_potential[:, None] - cost_tile) / epsilon, 0)
        row_potential = -epsilon * math.log(NN) - epsilon * log_sum_exp((col_potential[None, :] - cost_tile) / epsilon, 1)
    weights = jnp.exp((row_potential[:, None] + col_potential[None, :] - cost_tile) / epsilon + math.log(NN)).astype(jnp.bfloat16)
    target = jnp.zeros((NN, D), jnp.float32)
    for block in range(N_DP):
        lower = block * COLS_DEV
        part_k = jnp.dot(weights[:, lower:lower + COLS_DEV], latents[lower:lower + COLS_DEV], preferred_element_type=jnp.float32).astype(jnp.bfloat16)
        target = target + part_k.astype(jnp.float32)
    return row_potential, col_potential, target.astype(jnp.bfloat16)
```

```python
import math

import jax
import jax.numpy as jnp
from jax import lax
from jax.experimental import pallas as pl
from jax.experimental.pallas import tpu as pltpu
from jax.sharding import PartitionSpec as P

EPSILON = 0.01
NZ, NY, NX, NC = 8, 4, 4, 2
ROWS, COLS, D = 1024, 2048, 1024
NN, NM = 32768, 16384
A_COLS = 1280
LOG2E = math.log2(math.e)
NORM_SCALE = LOG2E / (EPSILON * D)
CROSS_SCALE = 2.0 * NORM_SCALE
STRIP = 256

BF = jnp.bfloat16
F32 = jnp.float32

GATHER = [
    ("Az", "p", 1), ("Az", "q", 1), ("Ay", "p", 1, 0), ("Ay", "q", 1, 0),
    ("Bz", "p", 1, 0), ("Bz", "q", 1, 0), ("By", "p", 1), ("By", "q", 1),
    ("Az", "p", 2), ("Ay", "p", 1, -1), ("Ay", "q", 1, -1), ("Az", "q", 2),
    ("Ay", "p", 1, 1), ("Ay", "q", 1, 1), ("Bz", "p", 2, 0), ("Bz", "q", 2, 0),
    ("Ay", "p", 2, 0), ("Bz", "p", 1, -1), ("Bz", "q", 1, -1), ("Bz", "p", 1, 1),
    ("Bz", "q", 1, 1), ("X", "p", 1), ("X", "q", 1), ("XS", 0), ("By", "p", 2), ("Az", "p", 3), ("Ay", "p", 1, -2),
    ("Ay", "q", 1, -2), ("Az", "q", 3), ("Ay", "p", 2, -1), ("Ay", "q", 1, 2),
    ("Bz", "p", 3, 0), ("Bz", "q", 3, 0), ("Ay", "p", 1, 2), ("Bz", "p", 2, -1),
    ("Bz", "q", 2, -1), ("Bz", "p", 2, 1), ("Bz", "q", 2, 1), ("X", "p", 2), ("XS", 1), ("XS", 2), ("Ay", "p", 2, 1),
    ("Bz", "q", 1, 2), ("Bz", "p", 1, 2), ("XS", 3), ("norm",), ("Ay", "p", 1, -3), ("Ay", "q", 1, -3),
    ("Az", "p", 4), ("Ay", "p", 2, -2), ("Ay", "q", 1, 3), ("dot", 0), ("Bz", "p", 4, 0),
    ("Bz", "q", 3, -1), ("Bz", "p", 3, -1), ("Ay", "p", 1, 3), ("Bz", "q", 3, 1),
    ("Bz", "p", 3, 1), ("Bz", "q", 2, 2), ("Bz", "p", 2, 2), ("Ay", "p", 2, 2), ("dot", 1),
    ("Bz", "p", 4, -1), ("Ay", "p", 2, -3), ("Ay", "q", 1, -4), ("Bz", "p", 4, 1),
    ("Ay", "p", 1, -4), ("Bz", "q", 3, 2), ("Bz", "p", 3, 2), ("dot", 2), ("Ay", "p", 2, 3),
    ("Ay", "p", 2, -4), ("Bz", "p", 4, 2),
]
DEPTH_PAIRS = ((0, -1), (1, -2), (2, -3), (3, -4))
KEYS = [e for e in GATHER if e[0] in ("Az", "Ay", "By", "Bz")]
SEM_OF = {k: i for i, k in enumerate(KEYS)}
XKEYS = [("X", "p", 1), ("X", "q", 1), ("X", "p", 2), ("XS", 0), ("XS", 1), ("XS", 2), ("XS", 3)]
XSEM_OF = {k: i for i, k in enumerate(XKEYS)}


def exp2(v):
    return jnp.exp2(v)


def kernel(noise_ref, lat_ref, row_out, col_out, tgt_out,
           lat_v, yt, xb, s_ref, e_ref, vy, sq, m_b, l_b, g_b, t_b, colw, roww,
           cx1, cx2, cx3, cs2, cs3, rx1, rx2, rx3, rs1, rs2, rs3,
           sib_s, sib_r, acc, far_s, far_r, near_s, near_r, mrg_s, mrg_r,
           in_sem, ysend, yrecv, xsend, xrecv, csend, crecv, rsend, rrecv, psend, precv, fsend, frecv):
    noise = lax.axis_index("noise")
    dp = lax.axis_index("dp")
    z, y = noise // NY, noise % NY
    x, c = dp // NC, dp % NC
    s = 1 - 2 * c

    def dev(zz, yy, xx, cc):
        return {"noise": zz * NY + yy, "dp": xx * NC + cc}

    def zat(k):
        return lax.rem(z + s * k + 2 * NZ, NZ)

    def yat(k):
        return lax.rem(y + s * k + 2 * NY, NY)

    def xat(k):
        return lax.rem(x + s * k + 2 * NX, NX)

    own_x = pl.multiple_of(dp * 128, 128)
    load_lat = pltpu.make_async_copy(lat_ref, lat_v, in_sem.at[0])
    load_x = pltpu.make_async_copy(noise_ref, xb.at[:, pl.ds(own_x, 128)], in_sem.at[1])
    load_lat.start()
    load_x.start()

    noise_peer = lambda k: lax.rem(noise + k, NZ * NY)
    dp_peer = lambda k: lax.rem(dp + k, NX * NC)
    barrier = pltpu.get_barrier_semaphore()
    for k in range(1, NZ * NY):
        pl.semaphore_signal(barrier, 1, device_id={"noise": noise_peer(k), "dp": dp})
    for k in range(1, NX * NC):
        pl.semaphore_signal(barrier, 1, device_id={"noise": noise, "dp": dp_peer(k)})

    def yrow(zz, yy):
        return pl.multiple_of(zz * 128 + yy * 32, 32)

    load_lat.wait()
    eye = (lax.broadcasted_iota(jnp.int32, (32, 32), 0) == lax.broadcasted_iota(jnp.int32, (32, 32), 1)).astype(F32).astype(BF)
    lat_t = lax.dot_general(eye, lat_v[...], (((1,), (1,)), ((), ())), preferred_element_type=F32)
    yt[pl.ds(yrow(z, y), 32), :] = lat_t.astype(BF)
    load_x.wait()
    pl.semaphore_wait(barrier, NZ * NY - 1 + NX * NC - 1)

    def xblk(xx, cc):
        return xb.at[:, pl.ds(pl.multiple_of((xx * NC + cc) * 128, 128), 128)]

    def sgn(pq):
        return 1 if pq == "p" else -1

    def desc(key):
        kind = key[0]
        if kind == "X":
            o = sgn(key[1])
            blk = xblk(xat(-o * (key[2] - 1)), c)
            to = dev(z, y, xat(o), c)
            sems = xsend, xrecv, XSEM_OF[key]
        elif kind == "XS":
            blk = xblk(xat((0, -1, 1, -2)[key[1]]), c)
            to = dev(z, y, x, 1 - c)
            sems = xsend, xrecv, XSEM_OF[key]
        else:
            o = sgn(key[1])
            if kind == "Az":
                blk = (zat(-o * (key[2] - 1)), y)
            elif kind == "Ay":
                blk = (zat(key[3]), yat(-o * (key[2] - 1)))
            elif kind == "By":
                blk = (z, yat(-o * (key[2] - 1)))
            else:
                blk = (zat(-o * (key[2] - 1)), yat(key[3]))
            cols = pl.ds(0, A_COLS) if kind[0] == "A" else pl.ds(A_COLS, COLS - A_COLS)
            blk = yt.at[pl.ds(yrow(*blk), 32), cols]
            to = dev(zat(o), y, x, c) if kind[1] == "z" else dev(z, yat(o), x, c)
            i = SEM_OF[key]
            return pltpu.make_async_remote_copy(
                src_ref=blk, dst_ref=blk, send_sem=ysend, recv_sem=yrecv.at[i],
                device_id=to, device_id_type=pl.DeviceIdType.MESH)
        i = sems[2]
        return pltpu.make_async_remote_copy(
            src_ref=blk, dst_ref=blk, send_sem=sems[0].at[i], recv_sem=sems[1].at[i],
            device_id=to, device_id_type=pl.DeviceIdType.MESH)

    def arrive(key):
        kind = key[0]
        if kind == "X":
            blk = xblk(xat(-sgn(key[1]) * key[2]), c)
            sem = xrecv.at[XSEM_OF[key]]
        elif kind == "XS":
            blk = xblk(xat((0, 1, -1, 2)[key[1]]), 1 - c)
            sem = xrecv.at[XSEM_OF[key]]
        else:
            o = sgn(key[1])
            if kind == "Az":
                blk = (zat(-o * key[2]), y)
            elif kind == "Ay":
                blk = (zat(key[3]), yat(-o * key[2]))
            elif kind == "By":
                blk = (z, yat(-o * key[2]))
            else:
                blk = (zat(-o * key[2]), yat(key[3]))
            cols = pl.ds(0, A_COLS) if kind[0] == "A" else pl.ds(A_COLS, COLS - A_COLS)
            blk = yt.at[pl.ds(yrow(*blk), 32), cols]
            sem = yrecv.at[SEM_OF[key]]
        pltpu.make_async_copy(blk, blk, sem).wait()

    def add_squares(blk_ref, first):
        v = blk_ref[...].astype(F32)
        sq[...] = v * v if first else sq[...] + v * v

    def depth_dot(pair, strip):
        cols = pl.ds(pl.multiple_of(strip * STRIP, STRIP), STRIP)
        rows = [pl.ds(pl.multiple_of(zat(k) * 128, 128), 128) for k in DEPTH_PAIRS[pair]]
        lhs = jnp.concatenate([xb[:, r] for r in rows], axis=1)
        rhs = jnp.concatenate([yt[r, cols] for r in rows], axis=0)
        return cols, CROSS_SCALE * jnp.dot(lhs, rhs, preferred_element_type=F32)

    def first_dot(strip, carry):
        cols, v = depth_dot(0, strip)
        a = m_b[...]
        s_ref[:, cols] = v + jnp.concatenate([a, a], axis=1)
        return carry

    def next_dot(pair):
        def body(strip, carry):
            cols, v = depth_dot(pair, strip)
            s_ref[:, cols] = s_ref[:, cols] + v
            return carry
        return body

    desc(("Az", "p", 1)).start()
    desc(("Az", "q", 1)).start()
    desc(("Ay", "p", 1, 0)).start()
    desc(("Ay", "q", 1, 0)).start()
    desc(("By", "p", 1)).start()
    desc(("By", "q", 1)).start()
    desc(("Bz", "p", 1, 0)).start()
    desc(("Bz", "q", 1, 0)).start()
    desc(("X", "p", 1)).start()
    desc(("X", "q", 1)).start()
    desc(("XS", 0)).start()
    add_squares(xblk(x, c), True)

    for key in GATHER:
        kind = key[0]
        if kind == "norm":
            m_b[...] = jnp.broadcast_to(-NORM_SCALE * jnp.sum(sq[...], axis=1, keepdims=True), (ROWS, 128))
            continue
        if kind == "dot":
            if key[1] == 0:
                lax.fori_loop(0, COLS // STRIP, first_dot, 0)
            else:
                lax.fori_loop(0, COLS // STRIP, next_dot(key[1]), 0)
            continue
        arrive(key)
        if kind == "Az":
            o = sgn(key[1])
            if key[2] < (4 if o == 1 else 3):
                desc(("Az", key[1], key[2] + 1)).start()
            desc(("Ay", "p", 1, -o * key[2])).start()
            desc(("Ay", "q", 1, -o * key[2])).start()
        elif kind == "Ay":
            if key[1] == "p" and key[2] == 1:
                desc(("Ay", "p", 2, key[3])).start()
        elif kind == "By":
            o = sgn(key[1])
            if key[1] == "p" and key[2] == 1:
                desc(("By", "p", 2)).start()
            yo = 2 if key[2] == 2 else -o
            desc(("Bz", "p", 1, yo)).start()
            desc(("Bz", "q", 1, yo)).start()
        elif kind == "Bz":
            if key[2] < (4 if key[1] == "p" else 3):
                desc(("Bz", key[1], key[2] + 1, key[3])).start()
        elif kind == "X":
            if key == ("X", "p", 1):
                desc(("X", "p", 2)).start()
            desc(("XS", {("p", 1): 1, ("q", 1): 2, ("p", 2): 3}[key[1:]])).start()
            add_squares(xblk(xat(-sgn(key[1]) * key[2]), c), False)
        elif kind == "XS":
            add_squares(xblk(xat((0, 1, -1, 2)[key[1]]), 1 - c), False)

    def last_dot(strip, carry):
        cols, v = depth_dot(3, strip)
        v = s_ref[:, cols] + v
        s_ref[:, cols] = v
        peak = jnp.max(jnp.max(v.reshape(ROWS // 8, 8, STRIP), axis=0), axis=0, keepdims=True)
        total = jnp.sum(jnp.sum(exp2(s_ref[:, cols] - peak).reshape(ROWS // 8, 8, STRIP), axis=0), axis=0, keepdims=True)
        lse = peak + jnp.log2(total)
        for h in range(STRIP // 128):
            colw[pl.ds(strip * (STRIP // 128) + h, 1), :] = lse[:, h * 128:(h + 1) * 128]
        return carry

    lax.fori_loop(0, COLS // STRIP, last_dot, 0)

    def to_all_noise(buf, i):
        for k in range(1, NZ * NY):
            pltpu.make_async_remote_copy(
                src_ref=buf.at[noise], dst_ref=buf.at[noise], send_sem=csend.at[i], recv_sem=crecv.at[i],
                device_id={"noise": noise_peer(k), "dp": dp}, device_id_type=pl.DeviceIdType.MESH).start()

    def from_all_noise(buf, i):
        part = buf.at[pl.ds(0, NZ * NY - 1)]
        pltpu.make_async_copy(part, part, crecv.at[i]).wait()

    def to_all_dp(buf, i):
        for k in range(1, NX * NC):
            pltpu.make_async_remote_copy(
                src_ref=buf.at[dp], dst_ref=buf.at[dp], send_sem=rsend.at[i], recv_sem=rrecv.at[i],
                device_id={"noise": noise, "dp": dp_peer(k)}, device_id_type=pl.DeviceIdType.MESH).start()

    def from_all_dp(buf, i):
        part = buf.at[pl.ds(0, NX * NC - 1)]
        pltpu.make_async_copy(part, part, rrecv.at[i]).wait()

    def row_of(ref, n):
        return jnp.concatenate([ref[k:k + 1, :] for k in range(n)], axis=1)

    def dense_into(ref, row, n):
        for k in range(n):
            ref[k:k + 1, :] = row[:, k * 128:(k + 1) * 128]

    def stacked(row):
        n = row.shape[1]
        hi = row.astype(BF).astype(F32)
        lo = row - hi
        i = lax.broadcasted_iota(jnp.int32, (16, n), 0)
        return jnp.where(i == 0, jnp.broadcast_to(hi, (16, n)), jnp.where(i == 1, jnp.broadcast_to(lo, (16, n)), 0.0)).astype(BF)

    def lse_of(buf):
        v = buf[...]
        peak = jnp.max(v, axis=0)
        return peak + jnp.log2(jnp.sum(exp2(v - peak[None]), axis=0))

    def spread(ref, out):
        for b in range(ROWS // 128):
            out[b * 128:(b + 1) * 128, :] = jnp.broadcast_to(ref[b:b + 1, :], (128, 128)).T

    cx1[noise] = colw[...]
    to_all_noise(cx1, 0)
    whole_y = yt.at[pl.ds(0, 992), :]
    pltpu.make_async_copy(whole_y, whole_y, ysend).wait()
    for i in range(len(XKEYS)):
        b = xblk(x, c)
        pltpu.make_async_copy(b, b, xsend.at[i]).wait()
    from_all_noise(cx1, 0)
    col1 = -math.log2(NM) - lse_of(cx1)
    colw[...] = col1

    col_row = row_of(colw, 16)

    def row_pass(i, carry):
        rows = pl.ds(pl.multiple_of(i * 32, 32), 32)
        v = s_ref[rows, :] + col_row
        peak = jnp.max(v, axis=1, keepdims=True)
        e = exp2(v - peak)
        total = jnp.sum(e, axis=1, keepdims=True)
        e_ref[rows, :] = e.astype(BF)
        m_b[rows, :] = jnp.broadcast_to(peak, (32, 128))
        l_b[rows, :] = jnp.broadcast_to(peak + jnp.log2(total), (32, 128))
        return carry

    lax.fori_loop(0, ROWS // 32, row_pass, 0)
    lane = lax.broadcasted_iota(jnp.int32, (128, 128), 1)
    for b in range(ROWS // 128):
        blk = pl.ds(b * 128, 128)
        t = jnp.where(lane == 0, m_b[blk, :], l_b[blk, :]).T
        roww[0, b:b + 1, :] = t[0:1, :]
        roww[1, b:b + 1, :] = t[1:2, :]
    rx1[dp] = roww[1]
    to_all_dp(rx1, 0)
    from_all_dp(rx1, 0)
    lse1 = lse_of(rx1)
    g = exp2(roww[0] - lse1)
    row1 = -math.log2(NN) - lse1
    roww[0] = g

    def col_sums(buf, stage, i, u):
        roww[1] = u
        q = jnp.dot(stacked(row_of(roww.at[1], 8)), e_ref[...], preferred_element_type=F32)
        dense_into(colw, q[0:1, :] + q[1:2, :], 16)
        stage[...] = colw[...]
        buf[noise] = stage[...].astype(BF)
        to_all_noise(buf, i)

    def row_sums(v, buf, i):
        colw[...] = v
        q = lax.dot_general(stacked(row_of(colw, 16)), e_ref[...], (((1,), (1,)), ((), ())), preferred_element_type=F32)
        dense_into(roww.at[1], q[0:1, :] + q[1:2, :], 8)
        buf[dp] = roww[1] * roww[0]
        to_all_dp(buf, i)

    col_sums(cx2, cs2, 1, g)
    spread(roww.at[0], g_b)
    norms = jnp.zeros((1, COLS), F32)
    def col_norm(i, carry):
        v = yt[pl.ds(pl.multiple_of(i * 32, 32), 32), :].astype(F32)
        return carry + jnp.sum((v * v).reshape(4, 8, COLS), axis=0)
    norms = jnp.sum(lax.fori_loop(0, D // 32, col_norm, jnp.zeros((8, COLS), F32)), axis=0, keepdims=True)
    dense_into(cs3, norms, 16)
    from_all_noise(cx2, 1)
    row_sums(1.0 / jnp.sum(cx2[...].astype(F32), axis=0), rx2, 1)
    from_all_dp(rx2, 1)
    t2 = jnp.sum(rx2[...], axis=0)

    col_sums(cx3, cs2, 2, roww[0] / t2)
    from_all_noise(cx3, 2)
    q3 = jnp.sum(cx3[...].astype(F32), axis=0)
    v3 = 1.0 / q3
    col_out[...] = (EPSILON / LOG2E) * (col1 + 2.0 - jnp.log2(q3) + NORM_SCALE * cs3[...])
    row_sums(v3, rx3, 2)
    v_row = row_of(colw, 16)

    def scale_latents(i, carry):
        rows = pl.ds(pl.multiple_of(i * 32, 32), 32)
        vy[rows, :] = (yt[rows, :].astype(F32) * v_row).astype(BF)
        return carry

    lax.fori_loop(0, D // 32, scale_latents, 0)

    half = pl.ds(0, ROWS // 2), pl.ds(ROWS // 2, ROWS // 2)
    right, left = dev(z, y, lax.rem(x + 1, NX), c), dev(z, y, lax.rem(x + NX - 1, NX), c)

    def rcopy(src, dst, i, to):
        return pltpu.make_async_remote_copy(
            src_ref=src, dst_ref=dst, send_sem=fsend.at[i], recv_sem=frecv.at[i],
            device_id=to, device_id_type=pl.DeviceIdType.MESH)

    def sib_copy(k):
        return pltpu.make_async_remote_copy(
            src_ref=sib_s.at[k], dst_ref=sib_r.at[k], send_sem=psend.at[k], recv_sem=precv.at[k],
            device_id=dev(z, y, x, 1 - c), device_id_type=pl.DeviceIdType.MESH)

    def weigh(k, step):
        xx = lax.rem(x + step, NX)
        w = vy.at[pl.ds(pl.multiple_of(xx * 256, 256), 256), :]

        def body(h, carry):
            rows = pl.ds(pl.multiple_of(h * 512, 512), 512)
            p = lax.dot_general(e_ref[rows, :], w[...], (((1,), (1,)), ((), ())), preferred_element_type=F32)
            gg = g_b[rows, :]
            lo, hi = p[:, :128] * gg, p[:, 128:] * gg
            acc[k, rows, :] = jnp.where(c == 0, lo, hi)
            sib_s[k, rows, :] = jnp.where(c == 0, hi, lo).astype(BF)
            return carry

        lax.fori_loop(0, 2, body, 0)
        sib_copy(k).start()

    def presum(k):
        sib_copy(k).wait_recv()
        return acc[k] + sib_r[k].astype(F32)

    weigh(0, 2)
    weigh(1, 1)
    far_s[...] = presum(0).astype(BF)
    far = [rcopy(far_s.at[half[0]], far_r.at[0], 0, right), rcopy(far_s.at[half[1]], far_r.at[1], 1, left)]
    for f in far:
        f.start()
    weigh(2, 3)
    acc[1] = presum(1)
    near_s[0] = acc[1, half[1], :].astype(BF)
    near0 = rcopy(near_s.at[0], near_r.at[0], 2, right)
    near0.start()
    weigh(3, 0)
    acc[2] = presum(2)
    near_s[1] = acc[2, half[0], :].astype(BF)
    near1 = rcopy(near_s.at[1], near_r.at[1], 3, left)
    near1.start()
    far[0].wait_recv()
    mrg_s[0] = (acc[1, half[0], :] + far_r[0].astype(F32)).astype(BF)
    mrg0 = rcopy(mrg_s.at[0], mrg_r.at[0], 4, right)
    mrg0.start()
    far[1].wait_recv()
    mrg_s[1] = (acc[2, half[1], :] + far_r[1].astype(F32)).astype(BF)
    mrg1 = rcopy(mrg_s.at[1], mrg_r.at[1], 5, left)
    mrg1.start()
    acc[3] = presum(3)
    from_all_dp(rx3, 2)
    t3 = jnp.sum(rx3[...], axis=0)
    row_out[...] = (EPSILON / LOG2E) * (row1 - 2.0 - jnp.log2(t3))
    roww[1] = 1.0 / t3
    spread(roww.at[1], t_b)
    near0.wait_recv()
    near1.wait_recv()
    mrg0.wait_recv()
    tgt_out[half[0], :] = ((acc[3, half[0], :] + near_r[1].astype(F32) + mrg_r[0].astype(F32)) * t_b[half[0], :]).astype(BF)
    mrg1.wait_recv()
    tgt_out[half[1], :] = ((acc[3, half[1], :] + near_r[0].astype(F32) + mrg_r[1].astype(F32)) * t_b[half[1], :]).astype(BF)

    for d in far + [near0, near1, mrg0, mrg1]:
        d.wait_send()
    for k in range(4):
        sib_copy(k).wait_send()
    for i, buf in enumerate((cx1, cx2, cx3)):
        part = buf.at[pl.ds(0, NZ * NY - 1)]
        pltpu.make_async_copy(part, part, csend.at[i]).wait()
    for i, buf in enumerate((rx1, rx2, rx3)):
        part = buf.at[pl.ds(0, NX * NC - 1)]
        pltpu.make_async_copy(part, part, rsend.at[i]).wait()


def local(noise_batch, latents):
    v = pltpu.VMEM
    dma = pltpu.SemaphoreType.DMA
    row, col, tgt = pl.pallas_call(
        kernel,
        out_shape=(
            jax.ShapeDtypeStruct((8, 128), F32),
            jax.ShapeDtypeStruct((16, 128), F32),
            jax.ShapeDtypeStruct((ROWS, 128), BF),
        ),
        in_specs=[pl.BlockSpec(memory_space=pl.ANY)] * 2,
        out_specs=[pl.BlockSpec(memory_space=pltpu.VMEM)] * 3,
        scratch_shapes=[
            v((COLS, 32), BF),
            v((D, COLS), BF),
            v((ROWS, D), BF),
            v((ROWS, COLS), F32),
            v((ROWS, COLS), BF),
            v((D, COLS), BF),
            v((ROWS, 128), F32),
            v((ROWS, 128), F32),
            v((ROWS, 128), F32),
            v((ROWS, 128), F32),
            v((ROWS, 128), F32),
            v((16, 128), F32),
            v((2, 8, 128), F32),
            v((32, 16, 128), F32),
            v((32, 16, 128), BF),
            v((32, 16, 128), BF),
            v((16, 128), F32),
            v((16, 128), F32),
            v((8, 8, 128), F32),
            v((8, 8, 128), F32),
            v((8, 8, 128), F32),
            v((8, 128), F32),
            v((8, 128), F32),
            v((8, 128), F32),
            v((4, ROWS, 128), BF),
            v((4, ROWS, 128), BF),
            v((4, ROWS, 128), F32),
            v((ROWS, 128), BF),
            v((2, ROWS // 2, 128), BF),
            v((2, ROWS // 2, 128), BF),
            v((2, ROWS // 2, 128), BF),
            v((2, ROWS // 2, 128), BF),
            v((2, ROWS // 2, 128), BF),
            dma((2,)),
            dma,
            dma((len(KEYS),)),
            dma((len(XKEYS),)),
            dma((len(XKEYS),)),
            dma((3,)),
            dma((3,)),
            dma((3,)),
            dma((3,)),
            dma((4,)),
            dma((4,)),
            dma((6,)),
            dma((6,)),
        ],
        compiler_params=pltpu.CompilerParams(
            collective_id=0, has_side_effects=True, vmem_limit_bytes=56 * 2**20),
        cost_estimate=pl.CostEstimate(flops=4 * ROWS * COLS * D, bytes_accessed=2**20, transcendentals=2 * ROWS * COLS),
    )(noise_batch, latents)
    return row.reshape(ROWS), col.reshape(COLS), tgt


def solution(mesh):
    in_specs = (P("noise", "dp"), P("dp", "noise"))
    out_specs = (P("noise"), P("dp"), P("noise", "dp"))
    return jax.shard_map(local, mesh=mesh, in_specs=in_specs, out_specs=out_specs, check_vma=False)
```

```python
import math

import jax
import jax.numpy as jnp
from jax import lax
from jax.experimental import pallas as pl
from jax.experimental.pallas import tpu as pltpu
from jax.sharding import PartitionSpec as P

EPSILON = 0.01
NZ, NY, NX, NC = 8, 4, 4, 2
ROWS, COLS, D = 1024, 2048, 1024
NN, NM = 32768, 16384
A_COLS = 1280
LOG2E = math.log2(math.e)
NORM_SCALE = LOG2E / (EPSILON * D)
CROSS_SCALE = 2.0 * NORM_SCALE
STRIP = 256

BF = jnp.bfloat16
F32 = jnp.float32

GATHER = [
    ("Az", "p", 1), ("Az", "q", 1), ("Ay", "p", 1, 0), ("Ay", "q", 1, 0),
    ("Bz", "p", 1, 0), ("Bz", "q", 1, 0), ("By", "p", 1), ("By", "q", 1),
    ("Az", "p", 2), ("Ay", "p", 1, -1), ("Ay", "q", 1, -1), ("Az", "q", 2),
    ("Ay", "p", 1, 1), ("Ay", "q", 1, 1), ("Bz", "p", 2, 0), ("Bz", "q", 2, 0),
    ("Ay", "p", 2, 0), ("Bz", "p", 1, -1), ("Bz", "q", 1, -1), ("Bz", "p", 1, 1),
    ("Bz", "q", 1, 1), ("X", "p", 1), ("X", "q", 1), ("XS", 0), ("By", "p", 2), ("Az", "p", 3), ("Ay", "p", 1, -2),
    ("Ay", "q", 1, -2), ("Az", "q", 3), ("Ay", "p", 2, -1), ("Ay", "q", 1, 2),
    ("Bz", "p", 3, 0), ("Bz", "q", 3, 0), ("Ay", "p", 1, 2), ("Bz", "p", 2, -1),
    ("Bz", "q", 2, -1), ("Bz", "p", 2, 1), ("Bz", "q", 2, 1), ("X", "p", 2), ("XS", 1), ("XS", 2), ("Ay", "p", 2, 1),
    ("Bz", "q", 1, 2), ("Bz", "p", 1, 2), ("XS", 3), ("norm",), ("Ay", "p", 1, -3), ("Ay", "q", 1, -3),
    ("Az", "p", 4), ("Ay", "p", 2, -2), ("Ay", "q", 1, 3), ("dot", 0), ("Bz", "p", 4, 0),
    ("Bz", "q", 3, -1), ("Bz", "p", 3, -1), ("Ay", "p", 1, 3), ("Bz", "q", 3, 1),
    ("Bz", "p", 3, 1), ("Bz", "q", 2, 2), ("Bz", "p", 2, 2), ("Ay", "p", 2, 2), ("dot", 1),
    ("Bz", "p", 4, -1), ("Ay", "p", 2, -3), ("Ay", "q", 1, -4), ("Bz", "p", 4, 1),
    ("Ay", "p", 1, -4), ("Bz", "q", 3, 2), ("Bz", "p", 3, 2), ("dot", 2), ("Ay", "p", 2, 3),
    ("Ay", "p", 2, -4), ("Bz", "p", 4, 2),
]
DEPTH_PAIRS = ((0, -1), (1, -2), (2, -3), (3, -4))
KEYS = [e for e in GATHER if e[0] in ("Az", "Ay", "By", "Bz")]
SEM_OF = {k: i for i, k in enumerate(KEYS)}
XKEYS = [("X", "p", 1), ("X", "q", 1), ("X", "p", 2), ("XS", 0), ("XS", 1), ("XS", 2), ("XS", 3)]
XSEM_OF = {k: i for i, k in enumerate(XKEYS)}

FAR_FIRST = sorted(
    ((dz, dy) for dz in range(-3, 5) for dy in range(-1, 3) if dz or dy),
    key=lambda p: (-abs(p[0]) - abs(p[1]), p))


def exp2(v):
    return jnp.exp2(v)


def kernel(noise_ref, lat_ref, row_out, col_out, tgt_out,
           yt, xb, s_ref, e_ref, vy, sq, m_b, l_b, g_b, t_b, colw, roww,
           cx1, cx2, cx3, cs2, cs3, rx1, rx2, rx3,
           sib_s, sib_r, acc, far_s, far_r, near_s, near_r, mrg_s, mrg_r,
           in_sem, ysend, yrecv, xsend, xrecv, csend, crecv, rsend, rrecv, psend, precv, fsend, frecv):
    noise = lax.axis_index("noise")
    dp = lax.axis_index("dp")
    z, y = noise // NY, noise % NY
    x, c = dp // NC, dp % NC
    s = 1 - 2 * c

    def dev(zz, yy, xx, cc):
        return {"noise": zz * NY + yy, "dp": xx * NC + cc}

    def zat(k):
        return lax.rem(z + s * k + 2 * NZ, NZ)

    def yat(k):
        return lax.rem(y + s * k + 2 * NY, NY)

    def xat(k):
        return lax.rem(x + s * k + 2 * NX, NX)

    def yrow(zz, yy):
        return pl.multiple_of(zz * 128 + yy * 32, 32)

    own_x = pl.multiple_of(dp * 128, 128)
    load_lat = pltpu.make_async_copy(lat_ref, yt.at[pl.ds(yrow(z, y), 32), :], in_sem.at[0])
    load_x = pltpu.make_async_copy(noise_ref, xb.at[:, pl.ds(own_x, 128)], in_sem.at[1])
    load_lat.start()
    load_x.start()

    MESH = pl.DeviceIdType.MESH
    barrier = pltpu.get_barrier_semaphore()
    around = [dev(zat(1), y, x, c), dev(zat(-1), y, x, c), dev(z, yat(1), x, c), dev(z, yat(-1), x, c),
              dev(z, y, xat(1), c), dev(z, y, xat(-1), c), dev(z, y, x, 1 - c)]
    for to in around:
        pl.semaphore_signal(barrier, 1, device_id=to, device_id_type=MESH)

    load_lat.wait()
    load_x.wait()
    pl.semaphore_wait(barrier, len(around))

    pending = []

    def finish():
        for part, sem in pending:
            pltpu.make_async_copy(part, part, sem).wait()

    def xblk(xx, cc):
        return xb.at[:, pl.ds(pl.multiple_of((xx * NC + cc) * 128, 128), 128)]

    def sgn(pq):
        return 1 if pq == "p" else -1

    def desc(key):
        kind = key[0]
        if kind == "X":
            o = sgn(key[1])
            blk = xblk(xat(-o * (key[2] - 1)), c)
            to = dev(z, y, xat(o), c)
            sems = xsend, xrecv, XSEM_OF[key]
        elif kind == "XS":
            blk = xblk(xat((0, -1, 1, -2)[key[1]]), c)
            to = dev(z, y, x, 1 - c)
            sems = xsend, xrecv, XSEM_OF[key]
        else:
            o = sgn(key[1])
            if kind == "Az":
                blk = (zat(-o * (key[2] - 1)), y)
            elif kind == "Ay":
                blk = (zat(key[3]), yat(-o * (key[2] - 1)))
            elif kind == "By":
                blk = (z, yat(-o * (key[2] - 1)))
            else:
                blk = (zat(-o * (key[2] - 1)), yat(key[3]))
            cols = pl.ds(0, A_COLS) if kind[0] == "A" else pl.ds(A_COLS, COLS - A_COLS)
            blk = yt.at[pl.ds(yrow(*blk), 32), cols]
            to = dev(zat(o), y, x, c) if kind[1] == "z" else dev(z, yat(o), x, c)
            i = SEM_OF[key]
            return pltpu.make_async_remote_copy(
                src_ref=blk, dst_ref=blk, send_sem=ysend, recv_sem=yrecv.at[i],
                device_id=to, device_id_type=pl.DeviceIdType.MESH)
        i = sems[2]
        return pltpu.make_async_remote_copy(
            src_ref=blk, dst_ref=blk, send_sem=sems[0].at[i], recv_sem=sems[1].at[i],
            device_id=to, device_id_type=pl.DeviceIdType.MESH)

    def arrive(key):
        kind = key[0]
        if kind == "X":
            blk = xblk(xat(-sgn(key[1]) * key[2]), c)
            sem = xrecv.at[XSEM_OF[key]]
        elif kind == "XS":
            blk = xblk(xat((0, 1, -1, 2)[key[1]]), 1 - c)
            sem = xrecv.at[XSEM_OF[key]]
        else:
            o = sgn(key[1])
            if kind == "Az":
                blk = (zat(-o * key[2]), y)
            elif kind == "Ay":
                blk = (zat(key[3]), yat(-o * key[2]))
            elif kind == "By":
                blk = (z, yat(-o * key[2]))
            else:
                blk = (zat(-o * key[2]), yat(key[3]))
            cols = pl.ds(0, A_COLS) if kind[0] == "A" else pl.ds(A_COLS, COLS - A_COLS)
            blk = yt.at[pl.ds(yrow(*blk), 32), cols]
            sem = yrecv.at[SEM_OF[key]]
        pltpu.make_async_copy(blk, blk, sem).wait()

    def add_squares(blk_ref, first):
        v = blk_ref[...].astype(F32)
        sq[...] = v * v if first else sq[...] + v * v

    def depth_dot(pair, strip):
        cols = pl.ds(pl.multiple_of(strip * STRIP, STRIP), STRIP)
        rows = [pl.ds(pl.multiple_of(zat(k) * 128, 128), 128) for k in DEPTH_PAIRS[pair]]
        lhs = jnp.concatenate([xb[:, r] for r in rows], axis=1)
        rhs = jnp.concatenate([yt[r, cols] for r in rows], axis=0)
        return cols, CROSS_SCALE * jnp.dot(lhs, rhs, preferred_element_type=F32)

    def first_dot(strip, carry):
        cols, v = depth_dot(0, strip)
        a = m_b[...]
        s_ref[:, cols] = v + jnp.concatenate([a, a], axis=1)
        return carry

    def next_dot(pair):
        def body(strip, carry):
            cols, v = depth_dot(pair, strip)
            s_ref[:, cols] = s_ref[:, cols] + v
            return carry
        return body

    desc(("Az", "p", 1)).start()
    desc(("Az", "q", 1)).start()
    desc(("Ay", "p", 1, 0)).start()
    desc(("Ay", "q", 1, 0)).start()
    desc(("By", "p", 1)).start()
    desc(("By", "q", 1)).start()
    desc(("Bz", "p", 1, 0)).start()
    desc(("Bz", "q", 1, 0)).start()
    desc(("X", "p", 1)).start()
    desc(("X", "q", 1)).start()
    desc(("XS", 0)).start()
    add_squares(xblk(x, c), True)

    for key in GATHER:
        kind = key[0]
        if kind == "norm":
            m_b[...] = jnp.broadcast_to(-NORM_SCALE * jnp.sum(sq[...], axis=1, keepdims=True), (ROWS, 128))
            continue
        if kind == "dot":
            if key[1] == 0:
                lax.fori_loop(0, COLS // STRIP, first_dot, 0)
            else:
                lax.fori_loop(0, COLS // STRIP, next_dot(key[1]), 0)
            continue
        arrive(key)
        if kind == "Az":
            o = sgn(key[1])
            if key[2] < (4 if o == 1 else 3):
                desc(("Az", key[1], key[2] + 1)).start()
            desc(("Ay", "p", 1, -o * key[2])).start()
            desc(("Ay", "q", 1, -o * key[2])).start()
        elif kind == "Ay":
            if key[1] == "p" and key[2] == 1:
                desc(("Ay", "p", 2, key[3])).start()
        elif kind == "By":
            o = sgn(key[1])
            if key[1] == "p" and key[2] == 1:
                desc(("By", "p", 2)).start()
            yo = 2 if key[2] == 2 else -o
            desc(("Bz", "p", 1, yo)).start()
            desc(("Bz", "q", 1, yo)).start()
        elif kind == "Bz":
            if key[2] < (4 if key[1] == "p" else 3):
                desc(("Bz", key[1], key[2] + 1, key[3])).start()
        elif kind == "X":
            if key == ("X", "p", 1):
                desc(("X", "p", 2)).start()
            desc(("XS", {("p", 1): 1, ("q", 1): 2, ("p", 2): 3}[key[1:]])).start()
            add_squares(xblk(xat(-sgn(key[1]) * key[2]), c), False)
        elif kind == "XS":
            add_squares(xblk(xat((0, 1, -1, 2)[key[1]]), 1 - c), False)

    pending.append((yt.at[pl.ds(0, len(KEYS) // 2 * 32), :], ysend))
    for i in range(len(XKEYS)):
        pending.append((xblk(x, c), xsend.at[i]))

    def last_dot(strip, carry):
        cols, v = depth_dot(3, strip)
        v = s_ref[:, cols] + v
        s_ref[:, cols] = v
        peak = jnp.max(jnp.max(v.reshape(ROWS // 8, 8, STRIP), axis=0), axis=0, keepdims=True)
        total = jnp.sum(jnp.sum(exp2(s_ref[:, cols] - peak).reshape(ROWS // 8, 8, STRIP), axis=0), axis=0, keepdims=True)
        lse = peak + jnp.log2(total)
        for h in range(STRIP // 128):
            colw[pl.ds(strip * (STRIP // 128) + h, 1), :] = lse[:, h * 128:(h + 1) * 128]
        return carry

    lax.fori_loop(0, COLS // STRIP, last_dot, 0)

    def to_all_noise(buf, i):
        for dz, dy in FAR_FIRST:
            pltpu.make_async_remote_copy(
                src_ref=buf.at[noise], dst_ref=buf.at[noise], send_sem=csend.at[i], recv_sem=crecv.at[i],
                device_id=dev(zat(dz), yat(dy), x, c), device_id_type=MESH).start()
        pending.append((buf.at[pl.ds(0, NZ * NY - 1)], csend.at[i]))

    def from_all_noise(buf, i):
        part = buf.at[pl.ds(0, NZ * NY - 1)]
        pltpu.make_async_copy(part, part, crecv.at[i]).wait()

    def to_all_dp(buf, i):
        for dx, dc in ((2, 0), (2, 1), (1, 0), (1, 1), (-1, 0), (-1, 1), (0, 1)):
            pltpu.make_async_remote_copy(
                src_ref=buf.at[dp], dst_ref=buf.at[dp], send_sem=rsend.at[i], recv_sem=rrecv.at[i],
                device_id=dev(z, y, xat(dx), 1 - c if dc else c), device_id_type=MESH).start()
        pending.append((buf.at[pl.ds(0, NX * NC - 1)], rsend.at[i]))

    def from_all_dp(buf, i):
        part = buf.at[pl.ds(0, NX * NC - 1)]
        pltpu.make_async_copy(part, part, rrecv.at[i]).wait()

    def row_of(ref, n):
        return jnp.concatenate([ref[k:k + 1, :] for k in range(n)], axis=1)

    def dense_into(ref, row, n):
        for k in range(n):
            ref[k:k + 1, :] = row[:, k * 128:(k + 1) * 128]

    def stacked(row):
        n = row.shape[1]
        hi = row.astype(BF).astype(F32)
        lo = row - hi
        i = lax.broadcasted_iota(jnp.int32, (16, n), 0)
        return jnp.where(i == 0, jnp.broadcast_to(hi, (16, n)), jnp.where(i == 1, jnp.broadcast_to(lo, (16, n)), 0.0)).astype(BF)

    def lse_of(buf):
        v = buf[...]
        peak = jnp.max(v, axis=0)
        return peak + jnp.log2(jnp.sum(exp2(v - peak[None]), axis=0))

    def spread(ref, out):
        for b in range(ROWS // 128):
            out[b * 128:(b + 1) * 128, :] = jnp.broadcast_to(ref[b:b + 1, :], (128, 128)).T

    cx1[noise] = colw[...]
    to_all_noise(cx1, 0)
    from_all_noise(cx1, 0)
    col1 = -math.log2(NM) - lse_of(cx1)
    colw[...] = col1

    col_row = row_of(colw, 16)

    def lane_tiles(v):
        return [v[:, k * 128:(k + 1) * 128] for k in range(COLS // 128)]

    def tree(op, parts):
        while len(parts) > 1:
            parts = [op(*parts[i:i + 2]) for i in range(0, len(parts), 2)]
        return parts[0]

    def row_peaks(i, carry):
        rows = pl.ds(pl.multiple_of(i * 16, 16), 16)
        l_b[rows, :] = tree(jnp.maximum, lane_tiles(s_ref[rows, :] + col_row))
        return carry

    lax.fori_loop(0, ROWS // 16, row_peaks, 0, unroll=4)
    for b in range(ROWS // 128):
        blk = pl.ds(b * 128, 128)
        t = l_b[blk, :]
        m_b[blk, :] = jnp.broadcast_to(jnp.max(t, axis=1, keepdims=True), (128, 128))
        roww[0, b:b + 1, :] = jnp.max(t.T, axis=0, keepdims=True)

    def row_exps(i, carry):
        rows = pl.ds(pl.multiple_of(i * 16, 16), 16)
        peak = m_b[rows, :]
        parts = [exp2(v - peak) for v in lane_tiles(s_ref[rows, :] + col_row)]
        for k, e in enumerate(parts):
            e_ref[rows, k * 128:(k + 1) * 128] = e.astype(BF)
        l_b[rows, :] = tree(jnp.add, parts)
        return carry

    lax.fori_loop(0, ROWS // 16, row_exps, 0, unroll=4)
    for b in range(ROWS // 128):
        t = l_b[b * 128:(b + 1) * 128, :].T
        roww[1, b:b + 1, :] = jnp.sum(t, axis=0, keepdims=True)
    roww[1] = roww[0] + jnp.log2(roww[1])
    rx1[dp] = roww[1]
    to_all_dp(rx1, 0)
    from_all_dp(rx1, 0)
    lse1 = lse_of(rx1)
    g = exp2(roww[0] - lse1)
    row1 = -math.log2(NN) - lse1
    roww[0] = g

    def col_sums(buf, stage, i, u):
        roww[1] = u
        q = jnp.dot(stacked(row_of(roww.at[1], 8)), e_ref[...], preferred_element_type=F32)
        dense_into(colw, q[0:1, :] + q[1:2, :], 16)
        stage[...] = colw[...]
        buf[noise] = stage[...].astype(BF)
        to_all_noise(buf, i)

    def row_sums(v, buf, i):
        colw[...] = v
        q = lax.dot_general(stacked(row_of(colw, 16)), e_ref[...], (((1,), (1,)), ((), ())), preferred_element_type=F32)
        dense_into(roww.at[1], q[0:1, :] + q[1:2, :], 8)
        buf[dp] = roww[1] * roww[0]
        to_all_dp(buf, i)

    col_sums(cx2, cs2, 1, g)
    spread(roww.at[0], g_b)
    norms = jnp.zeros((1, COLS), F32)
    def col_norm(i, carry):
        v = yt[pl.ds(pl.multiple_of(i * 32, 32), 32), :].astype(F32)
        return carry + jnp.sum((v * v).reshape(4, 8, COLS), axis=0)
    norms = jnp.sum(lax.fori_loop(0, D // 32, col_norm, jnp.zeros((8, COLS), F32)), axis=0, keepdims=True)
    dense_into(cs3, norms, 16)
    from_all_noise(cx2, 1)
    row_sums(1.0 / jnp.sum(cx2[...].astype(F32), axis=0), rx2, 1)
    from_all_dp(rx2, 1)
    t2 = jnp.sum(rx2[...], axis=0)

    col_sums(cx3, cs2, 2, roww[0] / t2)
    from_all_noise(cx3, 2)
    q3 = jnp.sum(cx3[...].astype(F32), axis=0)
    v3 = 1.0 / q3
    col_out[...] = (EPSILON / LOG2E) * (col1 + 2.0 - jnp.log2(q3) + NORM_SCALE * cs3[...])
    row_sums(v3, rx3, 2)
    v_row = row_of(colw, 16)

    def scale_latents(i, carry):
        rows = pl.ds(pl.multiple_of(i * 32, 32), 32)
        vy[rows, :] = (yt[rows, :].astype(F32) * v_row).astype(BF)
        return carry

    lax.fori_loop(0, D // 32, scale_latents, 0)

    half = pl.ds(0, ROWS // 2), pl.ds(ROWS // 2, ROWS // 2)
    right, left = dev(z, y, lax.rem(x + 1, NX), c), dev(z, y, lax.rem(x + NX - 1, NX), c)

    def rcopy(src, dst, i, to):
        return pltpu.make_async_remote_copy(
            src_ref=src, dst_ref=dst, send_sem=fsend.at[i], recv_sem=frecv.at[i],
            device_id=to, device_id_type=pl.DeviceIdType.MESH)

    def sib_copy(k):
        return pltpu.make_async_remote_copy(
            src_ref=sib_s.at[k], dst_ref=sib_r.at[k], send_sem=psend.at[k], recv_sem=precv.at[k],
            device_id=dev(z, y, x, 1 - c), device_id_type=pl.DeviceIdType.MESH)

    def weigh(k, step):
        xx = lax.rem(x + step, NX)
        w = vy.at[pl.ds(pl.multiple_of(xx * 256, 256), 256), :]

        def body(h, carry):
            rows = pl.ds(pl.multiple_of(h * 512, 512), 512)
            p = lax.dot_general(e_ref[rows, :], w[...], (((1,), (1,)), ((), ())), preferred_element_type=F32)
            gg = g_b[rows, :]
            lo, hi = p[:, :128] * gg, p[:, 128:] * gg
            acc[k, rows, :] = jnp.where(c == 0, lo, hi)
            sib_s[k, rows, :] = jnp.where(c == 0, hi, lo).astype(BF)
            return carry

        lax.fori_loop(0, 2, body, 0)
        sib_copy(k).start()

    def presum(k):
        sib_copy(k).wait_recv()
        return acc[k] + sib_r[k].astype(F32)

    weigh(0, 2)
    weigh(1, 1)
    far_s[...] = presum(0).astype(BF)
    far = [rcopy(far_s.at[half[0]], far_r.at[0], 0, right), rcopy(far_s.at[half[1]], far_r.at[1], 1, left)]
    for f in far:
        f.start()
    weigh(2, 3)
    acc[1] = presum(1)
    near_s[0] = acc[1, half[1], :].astype(BF)
    near0 = rcopy(near_s.at[0], near_r.at[0], 2, right)
    near0.start()
    weigh(3, 0)
    acc[2] = presum(2)
    near_s[1] = acc[2, half[0], :].astype(BF)
    near1 = rcopy(near_s.at[1], near_r.at[1], 3, left)
    near1.start()
    far[0].wait_recv()
    mrg_s[0] = (acc[1, half[0], :] + far_r[0].astype(F32)).astype(BF)
    mrg0 = rcopy(mrg_s.at[0], mrg_r.at[0], 4, right)
    mrg0.start()
    far[1].wait_recv()
    mrg_s[1] = (acc[2, half[1], :] + far_r[1].astype(F32)).astype(BF)
    mrg1 = rcopy(mrg_s.at[1], mrg_r.at[1], 5, left)
    mrg1.start()
    acc[3] = presum(3)
    from_all_dp(rx3, 2)
    t3 = jnp.sum(rx3[...], axis=0)
    row_out[...] = (EPSILON / LOG2E) * (row1 - 2.0 - jnp.log2(t3))
    roww[1] = 1.0 / t3
    spread(roww.at[1], t_b)
    near0.wait_recv()
    near1.wait_recv()
    mrg0.wait_recv()
    tgt_out[half[0], :] = ((acc[3, half[0], :] + near_r[1].astype(F32) + mrg_r[0].astype(F32)) * t_b[half[0], :]).astype(BF)
    mrg1.wait_recv()
    tgt_out[half[1], :] = ((acc[3, half[1], :] + near_r[0].astype(F32) + mrg_r[1].astype(F32)) * t_b[half[1], :]).astype(BF)

    for d in far + [near0, near1, mrg0, mrg1]:
        d.wait_send()
    for k in range(4):
        sib_copy(k).wait_send()
    finish()


def place(row_in, col_in, tgt_in, row_out, col_out, tgt_out):
    row_out[...] = row_in[...]
    col_out[...] = col_in[...]
    tgt_out[...] = tgt_in[...]


def local(noise_batch, latents):
    v = pltpu.VMEM
    dma = pltpu.SemaphoreType.DMA
    row, col, tgt = pl.pallas_call(
        kernel,
        out_shape=(
            jax.ShapeDtypeStruct((8, 128), F32),
            jax.ShapeDtypeStruct((16, 128), F32),
            jax.ShapeDtypeStruct((ROWS, 128), BF),
        ),
        in_specs=[pl.BlockSpec(memory_space=pl.ANY)] * 2,
        out_specs=[pl.BlockSpec(memory_space=pltpu.VMEM)] * 3,
        scratch_shapes=[
            v((D, COLS), BF),
            v((ROWS, D), BF),
            v((ROWS, COLS), F32),
            v((ROWS, COLS), BF),
            v((D, COLS), BF),
            v((ROWS, 128), F32),
            v((ROWS, 128), F32),
            v((ROWS, 128), F32),
            v((ROWS, 128), F32),
            v((ROWS, 128), F32),
            v((16, 128), F32),
            v((2, 8, 128), F32),
            v((32, 16, 128), F32),
            v((32, 16, 128), BF),
            v((32, 16, 128), BF),
            v((16, 128), F32),
            v((16, 128), F32),
            v((8, 8, 128), F32),
            v((8, 8, 128), F32),
            v((8, 8, 128), F32),
            v((4, ROWS, 128), BF),
            v((4, ROWS, 128), BF),
            v((4, ROWS, 128), F32),
            v((ROWS, 128), BF),
            v((2, ROWS // 2, 128), BF),
            v((2, ROWS // 2, 128), BF),
            v((2, ROWS // 2, 128), BF),
            v((2, ROWS // 2, 128), BF),
            v((2, ROWS // 2, 128), BF),
            dma((2,)),
            dma,
            dma((len(KEYS),)),
            dma((len(XKEYS),)),
            dma((len(XKEYS),)),
            dma((3,)),
            dma((3,)),
            dma((3,)),
            dma((3,)),
            dma((4,)),
            dma((4,)),
            dma((6,)),
            dma((6,)),
        ],
        compiler_params=pltpu.CompilerParams(
            collective_id=0, has_side_effects=True, vmem_limit_bytes=56 * 2**20),
        cost_estimate=pl.CostEstimate(flops=4 * ROWS * COLS * D, bytes_accessed=2**20, transcendentals=2 * ROWS * COLS),
    )(noise_batch, latents.T)
    row, col, tgt = pl.pallas_call(
        place,
        out_shape=(
            jax.ShapeDtypeStruct((8, 128), F32),
            jax.ShapeDtypeStruct((16, 128), F32),
            jax.ShapeDtypeStruct((ROWS, 128), BF),
        ),
        in_specs=[pl.BlockSpec(memory_space=pltpu.VMEM)] * 3,
        out_specs=[pl.BlockSpec(memory_space=pltpu.VMEM)] * 3,
        compiler_params=pltpu.CompilerParams(vmem_limit_bytes=60 * 2**20),
    )(row, col, tgt)
    return row.reshape(ROWS), col.reshape(COLS), tgt


def solution(mesh):
    in_specs = (P("noise", "dp"), P("dp", "noise"))
    out_specs = (P("noise"), P("dp"), P("noise", "dp"))
    return jax.shard_map(local, mesh=mesh, in_specs=in_specs, out_specs=out_specs, check_vma=False)
```

```python
import math

import jax
import jax.numpy as jnp
from jax import lax
from jax.experimental import pallas as pl
from jax.experimental.pallas import tpu as pltpu
from jax.sharding import PartitionSpec as P

EPSILON = 0.01
NZ, NY, NX, NC = 8, 4, 4, 2
ROWS, COLS, D = 1024, 2048, 1024
NN, NM = 32768, 16384
LOG2E = math.log2(math.e)
NORM_SCALE = LOG2E / (EPSILON * D)
CROSS_SCALE = 2.0 * NORM_SCALE
STRIP = 256

BF = jnp.bfloat16
F32 = jnp.float32

HELD_AT = {
    'Az': {('p', 1): 0, ('p', 2): 1, ('p', 3): 2, ('p', 4): 3, ('q', 1): 0, ('q', 2): 1, ('q', 3): 2},
    'By': {('p', 1): 0, ('q', 1): 0, ('p', 2): 1},
    'Ay': {('p', 1): 0, ('q', 1): 0, ('p', 2): 1},
    'Bz': {('p', 1): 0, ('p', 2): 1, ('p', 3): 2, ('p', 4): 3, ('q', 1): 0, ('q', 2): 1, ('q', 3): 2},
}
GROUPS = (('A', 0, 768), ('B', 768, 256), ('A', 1024, 512), ('B', 1536, 512))
GATHER = (
    ('go', 0), ('go', 1), ('go', 2), ('go', 3), ('XS', 0), ('Az', 0, 'p', 1), ('Az', 0, 'q', 1), ('Ay', 0, 'p', 1, 0),
    ('Ay', 0, 'q', 1, 0), ('Bz', 1, 'p', 1, 0), ('Bz', 1, 'q', 1, 0), ('By', 1, 'p', 1), ('By', 1, 'q', 1),
    ('Az', 2, 'p', 1), ('Az', 2, 'q', 1), ('Ay', 2, 'p', 1, 0), ('Ay', 2, 'q', 1, 0), ('Bz', 3, 'p', 1, 0),
    ('Bz', 3, 'q', 1, 0), ('By', 3, 'p', 1), ('By', 3, 'q', 1), ('Az', 0, 'p', 2), ('Ay', 0, 'p', 1, -1),
    ('Ay', 0, 'q', 1, -1), ('Az', 0, 'q', 2), ('Ay', 0, 'p', 1, 1), ('Ay', 0, 'q', 1, 1), ('Bz', 1, 'p', 2, 0),
    ('Bz', 1, 'q', 2, 0), ('Bz', 1, 'p', 1, -1), ('X', 'p', 1), ('Bz', 1, 'q', 1, -1), ('X', 'q', 1),
    ('Bz', 1, 'p', 1, 1), ('Ay', 0, 'p', 2, 0), ('Bz', 1, 'q', 1, 1), ('Az', 2, 'p', 2), ('Az', 2, 'q', 2),
    ('By', 1, 'p', 2), ('XS', 1), ('Bz', 3, 'p', 2, 0), ('Ay', 2, 'p', 1, -1), ('XS', 2), ('Ay', 2, 'q', 1, -1),
    ('Bz', 3, 'q', 2, 0), ('Bz', 3, 'p', 1, -1), ('Ay', 2, 'p', 1, 1), ('Ay', 2, 'q', 1, 1), ('Bz', 3, 'q', 1, -1),
    ('Bz', 3, 'p', 1, 1), ('Ay', 2, 'p', 2, 0), ('Bz', 3, 'q', 1, 1), ('By', 3, 'p', 2), ('Az', 0, 'p', 3),
    ('Ay', 0, 'p', 1, -2), ('Ay', 0, 'q', 1, -2), ('Az', 0, 'q', 3), ('Ay', 0, 'p', 2, -1), ('Ay', 0, 'q', 1, 2),
    ('Bz', 1, 'p', 3, 0), ('Bz', 1, 'q', 3, 0), ('Bz', 1, 'p', 2, -1), ('Bz', 1, 'q', 2, -1), ('Bz', 1, 'p', 2, 1),
    ('Ay', 0, 'p', 1, 2), ('Bz', 1, 'q', 2, 1), ('Az', 2, 'p', 3), ('Az', 2, 'q', 3), ('Ay', 0, 'p', 2, 1),
    ('Bz', 1, 'q', 1, 2), ('X', 'p', 2), ('Bz', 1, 'p', 1, 2), ('Bz', 3, 'p', 3, 0), ('Ay', 2, 'p', 1, -2),
    ('Ay', 2, 'q', 1, -2), ('Bz', 3, 'q', 3, 0), ('Bz', 3, 'p', 2, -1), ('Ay', 2, 'p', 1, 2), ('Ay', 2, 'q', 1, 2),
    ('Bz', 3, 'q', 2, -1), ('Bz', 3, 'p', 2, 1), ('Bz', 3, 'q', 2, 1), ('XS', 3), ('norm',), ('Ay', 2, 'p', 2, -1),
    ('Ay', 2, 'p', 2, 1), ('Bz', 3, 'q', 1, 2), ('Bz', 3, 'p', 1, 2), ('Ay', 0, 'p', 1, -3), ('Ay', 0, 'q', 1, -3),
    ('Ay', 0, 'p', 2, -2), ('Ay', 0, 'q', 1, 3), ('Az', 0, 'p', 4), ('Bz', 1, 'p', 4, 0), ('Bz', 1, 'q', 3, -1),
    ('Bz', 1, 'p', 3, -1), ('Ay', 0, 'p', 1, 3), ('Bz', 1, 'q', 3, 1), ('Bz', 1, 'p', 3, 1), ('Bz', 1, 'q', 2, 2),
    ('Az', 2, 'p', 4), ('Bz', 1, 'p', 2, 2), ('dot', 0, 0), ('Bz', 3, 'p', 4, 0), ('dot', 0, 1), ('Ay', 0, 'p', 2, 2),
    ('Bz', 3, 'q', 3, -1), ('Bz', 3, 'p', 3, -1), ('Ay', 2, 'p', 1, -3), ('Ay', 2, 'q', 1, -3), ('dot', 0, 2),
    ('Bz', 3, 'q', 3, 1), ('Bz', 3, 'p', 3, 1), ('Ay', 2, 'p', 1, 3), ('Ay', 2, 'q', 1, 3), ('Bz', 3, 'q', 2, 2),
    ('dot', 0, 3), ('Bz', 3, 'p', 2, 2), ('Ay', 2, 'p', 2, -2), ('Ay', 2, 'p', 2, 2), ('dot', 0, 4),
    ('Bz', 1, 'p', 4, -1), ('Bz', 1, 'p', 4, 1), ('Bz', 1, 'p', 3, 2), ('dot', 0, 5), ('Ay', 0, 'p', 2, -3),
    ('Ay', 0, 'q', 1, -4), ('Bz', 1, 'q', 3, 2), ('Ay', 0, 'p', 1, -4), ('dot', 0, 6), ('Bz', 3, 'p', 4, -1),
    ('Bz', 3, 'p', 4, 1), ('Ay', 0, 'p', 2, 3), ('dot', 0, 7), ('Bz', 3, 'q', 3, 2), ('Ay', 2, 'p', 1, -4),
    ('Bz', 3, 'p', 3, 2), ('Ay', 2, 'q', 1, -4), ('Ay', 2, 'p', 2, -3), ('Bz', 1, 'p', 4, 2), ('Ay', 2, 'p', 2, 3),
    ('Ay', 0, 'p', 2, -4), ('dot', 1, 0), ('Ay', 2, 'p', 2, -4), ('dot', 1, 1), ('Bz', 3, 'p', 4, 2), ('dot', 1, 2),
    ('dot', 1, 3), ('dot', 1, 4), ('dot', 1, 5), ('dot', 1, 6), ('dot', 1, 7),
)
DEPTHS = ((0, -1, 1, -2), (2, -3, 3, -4))
KEYS = [e for e in GATHER if e[0] in ("Az", "Ay", "By", "Bz")]
assert len(set(KEYS)) == len(KEYS) == 31 * len(GROUPS)
SEM_OF = {k: i for i, k in enumerate(KEYS)}
XKEYS = [("X", "p", 1), ("X", "q", 1), ("X", "p", 2), ("XS", 0), ("XS", 1), ("XS", 2), ("XS", 3)]
XSEM_OF = {k: i for i, k in enumerate(XKEYS)}

FAR_FIRST = sorted(
    ((dz, dy) for dz in range(-3, 5) for dy in range(-1, 3) if dz or dy),
    key=lambda p: (-abs(p[0]) - abs(p[1]), p))


def exp2(v):
    return jnp.exp2(v)


def kernel(noise_ref, lat_ref, row_out, col_out, tgt_out,
           yt, xb, s_ref, e_ref, vy, sq, m_b, l_b, g_b, t_b, colw, roww,
           cx1, cx2, cx3, cx4, cs2, cs3, rx1, rx2, rx3,
           sib_s, sib_r, acc, far_s, far_r, near_s, near_r, mrg_s, mrg_r,
           in_sem, ysend, yrecv, xsend, xrecv, csend, crecv, rsend, rrecv, psend, precv, fsend, frecv):
    noise = lax.axis_index("noise")
    dp = lax.axis_index("dp")
    z, y = noise // NY, noise % NY
    x, c = dp // NC, dp % NC
    s = 1 - 2 * c

    def dev(zz, yy, xx, cc):
        return {"noise": zz * NY + yy, "dp": xx * NC + cc}

    def zat(k):
        return lax.rem(z + s * k + 2 * NZ, NZ)

    def yat(k):
        return lax.rem(y + s * k + 2 * NY, NY)

    def xat(k):
        return lax.rem(x + s * k + 2 * NX, NX)

    def yrow(zz, yy):
        return pl.multiple_of(zz * 128 + yy * 32, 32)

    own_x = pl.multiple_of(dp * 128, 128)
    load_lat = pltpu.make_async_copy(lat_ref, yt.at[pl.ds(yrow(z, y), 32), :], in_sem.at[0])
    load_x = pltpu.make_async_copy(noise_ref, xb.at[:, pl.ds(own_x, 128)], in_sem.at[1])
    load_lat.start()
    load_x.start()

    MESH = pl.DeviceIdType.MESH
    barrier = pltpu.get_barrier_semaphore()
    around = [dev(zat(1), y, x, c), dev(zat(-1), y, x, c), dev(z, yat(1), x, c), dev(z, yat(-1), x, c),
              dev(z, y, xat(1), c), dev(z, y, xat(-1), c), dev(z, y, x, 1 - c)]
    for to in around:
        pl.semaphore_signal(barrier, 1, device_id=to, device_id_type=MESH)

    load_lat.wait()
    load_x.wait()
    pl.semaphore_wait(barrier, len(around))

    pending = []

    def finish():
        for part, sem in pending:
            pltpu.make_async_copy(part, part, sem).wait()

    def xblk(xx, cc):
        return xb.at[:, pl.ds(pl.multiple_of((xx * NC + cc) * 128, 128), 128)]

    def sgn(pq):
        return 1 if pq == "p" else -1

    def block(key, dist):
        kind, g, o = key[0], key[1], sgn(key[2])
        if kind == "Az":
            at = zat(-o * dist), y
        elif kind == "Ay":
            at = zat(key[4]), yat(-o * dist)
        elif kind == "By":
            at = z, yat(-o * dist)
        else:
            at = zat(-o * dist), yat(key[4])
        return yt.at[pl.ds(yrow(*at), 32), pl.ds(GROUPS[g][1], GROUPS[g][2])]

    def desc(key):
        kind = key[0]
        if kind == "X":
            o = sgn(key[1])
            blk = xblk(xat(-o * (key[2] - 1)), c)
            to = dev(z, y, xat(o), c)
            sems = xsend, xrecv, XSEM_OF[key]
        elif kind == "XS":
            blk = xblk(xat((0, -1, 1, -2)[key[1]]), c)
            to = dev(z, y, x, 1 - c)
            sems = xsend, xrecv, XSEM_OF[key]
        else:
            o = sgn(key[2])
            held = HELD_AT[kind][key[2:4]]
            blk = block(key, held)
            step = o * (key[3] - held)
            to = dev(zat(step), y, x, c) if kind[1] == "z" else dev(z, yat(step), x, c)
            return pltpu.make_async_remote_copy(
                src_ref=blk, dst_ref=blk, send_sem=ysend, recv_sem=yrecv.at[SEM_OF[key]],
                device_id=to, device_id_type=MESH)
        i = sems[2]
        return pltpu.make_async_remote_copy(
            src_ref=blk, dst_ref=blk, send_sem=sems[0].at[i], recv_sem=sems[1].at[i],
            device_id=to, device_id_type=pl.DeviceIdType.MESH)

    def arrive(key):
        kind = key[0]
        if kind == "X":
            blk = xblk(xat(-sgn(key[1]) * key[2]), c)
            sem = xrecv.at[XSEM_OF[key]]
        elif kind == "XS":
            blk = xblk(xat((0, 1, -1, 2)[key[1]]), 1 - c)
            sem = xrecv.at[XSEM_OF[key]]
        else:
            blk = block(key, key[3])
            sem = yrecv.at[SEM_OF[key]]
        pltpu.make_async_copy(blk, blk, sem).wait()

    def add_squares(blk_ref, first):
        v = blk_ref[...].astype(F32)
        sq[...] = v * v if first else sq[...] + v * v

    def dot_strip(half, strip):
        cols = pl.ds(pl.multiple_of(strip * STRIP, STRIP), STRIP)
        rows = [pl.ds(pl.multiple_of(zat(k) * 128, 128), 128) for k in DEPTHS[half]]
        lhs = jnp.concatenate([xb[:, r] for r in rows], axis=1)
        rhs = jnp.concatenate([yt[r, cols] for r in rows], axis=0)
        v = CROSS_SCALE * jnp.dot(lhs, rhs, preferred_element_type=F32)
        if half == 0:
            a = m_b[...]
            s_ref[:, cols] = v + jnp.concatenate([a, a], axis=1)
            return
        v = s_ref[:, cols] + v
        s_ref[:, cols] = v
        peak = jnp.max(jnp.max(v.reshape(ROWS // 8, 8, STRIP), axis=0), axis=0, keepdims=True)
        total = jnp.zeros((8, STRIP), F32)
        for r in range(0, ROWS, 256):
            e = exp2(s_ref[r:r + 256, cols] - peak)
            total = total + jnp.sum(e.reshape(32, 8, STRIP), axis=0)
        lse = peak + jnp.log2(jnp.sum(total, axis=0, keepdims=True))
        for h in range(STRIP // 128):
            colw[pl.ds(strip * (STRIP // 128) + h, 1), :] = lse[:, h * 128:(h + 1) * 128]

    def dense_into(ref, row, n):
        for k in range(n):
            ref[k:k + 1, :] = row[:, k * 128:(k + 1) * 128]

    def to_all_noise(buf, i):
        for dz, dy in FAR_FIRST:
            pltpu.make_async_remote_copy(
                src_ref=buf.at[noise], dst_ref=buf.at[noise], send_sem=csend.at[i], recv_sem=crecv.at[i],
                device_id=dev(zat(dz), yat(dy), x, c), device_id_type=MESH).start()

    def from_all_noise(buf, i):
        part = buf.at[pl.ds(0, NZ * NY - 1)]
        pltpu.make_async_copy(part, part, crecv.at[i]).wait()

    desc(("X", "p", 1)).start()
    desc(("X", "q", 1)).start()
    desc(("XS", 0)).start()
    add_squares(xblk(x, c), True)

    def send_on(kind, g, held, slot=(), only="pq"):
        for o in only:
            for (direction, dist), at in HELD_AT[kind].items():
                if direction == o and at == held:
                    desc((kind, g, o, dist) + slot).start()

    def handle(key):
        kind = key[0]
        if kind == "norm":
            m_b[...] = jnp.broadcast_to(-NORM_SCALE * jnp.sum(sq[...], axis=1, keepdims=True), (ROWS, 128))
            return
        if kind == "go":
            g = key[1]
            near, far = ("Az", "Ay") if GROUPS[g][0] == "A" else ("By", "Bz")
            send_on(near, g, 0)
            send_on(far, g, 0, (0,))
            return
        arrive(key)
        if kind in ("Az", "By"):
            g, pq, d = key[1:]
            send_on(kind, g, d, only=pq)
            if kind == "Az":
                send_on("Ay", g, 0, (-sgn(pq) * d,))
            else:
                send_on("Bz", g, 0, (2 if d == 2 else -sgn(pq),))
        elif kind in ("Ay", "Bz"):
            g, pq, d, slot = key[1:]
            send_on(kind, g, d, (slot,), only=pq)
        elif kind == "X":
            if key == ("X", "p", 1):
                desc(("X", "p", 2)).start()
            desc(("XS", {("p", 1): 1, ("q", 1): 2, ("p", 2): 3}[key[1:]])).start()
            add_squares(xblk(xat(-sgn(key[1]) * key[2]), c), False)
        elif kind == "XS":
            add_squares(xblk(xat((0, 1, -1, 2)[key[1]]), 1 - c), False)

    ahead, steps_now = [], []
    for key in GATHER:
        if key[0] == "dot":
            ahead.append((key[1:], steps_now))
            steps_now = []
        else:
            steps_now.append(key)
    strips = COLS // STRIP
    assert [k for k, _ in ahead] == [(h, i) for h in range(2) for i in range(strips)] and not steps_now

    for half_no in range(2):
        def strip_body(i, carry, half_no=half_no):
            for j in range(strips):
                todo = ahead[half_no * strips + j][1]
                if todo and (half_no, j) != (0, 0):
                    @pl.when(i == j)
                    def _():
                        for key in todo:
                            handle(key)
            if half_no:
                @pl.when(i == strips // 2)
                def _():
                    cx1[noise] = colw[0:8, :]
                    to_all_noise(cx1, 0)
            dot_strip(half_no, i)
            return carry

        if half_no == 0:
            for key in ahead[0][1]:
                handle(key)
        lax.fori_loop(0, strips, strip_body, 0)
    cx4[noise] = colw[8:16, :]
    to_all_noise(cx4, 3)
    pending.append((cx1.at[pl.ds(0, NZ * NY - 1)], csend.at[0]))
    pending.append((cx4.at[pl.ds(0, NZ * NY - 1)], csend.at[3]))
    pending.append((yt.at[pl.ds(0, (NZ * NY - 1) * 32), pl.ds(0, sum(g[2] for g in GROUPS))], ysend))
    for i in range(len(XKEYS)):
        pending.append((xblk(x, c), xsend.at[i]))

    def to_all_dp(buf, i):
        for dx, dc in ((2, 0), (2, 1), (1, 0), (1, 1), (-1, 0), (-1, 1), (0, 1)):
            pltpu.make_async_remote_copy(
                src_ref=buf.at[dp], dst_ref=buf.at[dp], send_sem=rsend.at[i], recv_sem=rrecv.at[i],
                device_id=dev(z, y, xat(dx), 1 - c if dc else c), device_id_type=MESH).start()
        pending.append((buf.at[pl.ds(0, NX * NC - 1)], rsend.at[i]))

    def from_all_dp(buf, i):
        part = buf.at[pl.ds(0, NX * NC - 1)]
        pltpu.make_async_copy(part, part, rrecv.at[i]).wait()

    def row_of(ref, n):
        return jnp.concatenate([ref[k:k + 1, :] for k in range(n)], axis=1)

    def stacked(row):
        n = row.shape[1]
        hi = row.astype(BF).astype(F32)
        lo = row - hi
        i = lax.broadcasted_iota(jnp.int32, (16, n), 0)
        return jnp.where(i == 0, jnp.broadcast_to(hi, (16, n)), jnp.where(i == 1, jnp.broadcast_to(lo, (16, n)), 0.0)).astype(BF)

    def lse_of(buf):
        v = buf[...]
        peak = jnp.max(v, axis=0)
        return peak + jnp.log2(jnp.sum(exp2(v - peak[None]), axis=0))

    def spread(ref, out):
        for b in range(ROWS // 128):
            out[b * 128:(b + 1) * 128, :] = jnp.broadcast_to(ref[b:b + 1, :], (128, 128)).T

    from_all_noise(cx1, 0)
    lse_a = lse_of(cx1)
    from_all_noise(cx4, 3)
    lse_b = lse_of(cx4)
    colw[0:8, :] = lse_a
    colw[8:16, :] = lse_b
    col1 = -math.log2(NM) - colw[...]
    colw[...] = col1

    col_row = row_of(colw, 16)

    def lane_tiles(v):
        return [v[:, k * 128:(k + 1) * 128] for k in range(COLS // 128)]

    def tree(op, parts):
        while len(parts) > 1:
            parts = [op(*parts[i:i + 2]) for i in range(0, len(parts), 2)]
        return parts[0]

    def row_peaks(i, carry):
        rows = pl.ds(pl.multiple_of(i * 16, 16), 16)
        l_b[rows, :] = tree(jnp.maximum, lane_tiles(s_ref[rows, :] + col_row))
        return carry

    lax.fori_loop(0, ROWS // 16, row_peaks, 0, unroll=4)
    for b in range(ROWS // 128):
        blk = pl.ds(b * 128, 128)
        t = l_b[blk, :]
        m_b[blk, :] = jnp.broadcast_to(jnp.max(t, axis=1, keepdims=True), (128, 128))
        roww[0, b:b + 1, :] = jnp.max(t.T, axis=0, keepdims=True)

    def row_exps(i, carry):
        rows = pl.ds(pl.multiple_of(i * 16, 16), 16)
        peak = m_b[rows, :]
        parts = [exp2(v - peak) for v in lane_tiles(s_ref[rows, :] + col_row)]
        for k, e in enumerate(parts):
            e_ref[rows, k * 128:(k + 1) * 128] = e.astype(BF)
        l_b[rows, :] = tree(jnp.add, parts)
        return carry

    lax.fori_loop(0, ROWS // 16, row_exps, 0, unroll=4)
    for b in range(ROWS // 128):
        t = l_b[b * 128:(b + 1) * 128, :].T
        roww[1, b:b + 1, :] = jnp.sum(t, axis=0, keepdims=True)
    roww[1] = roww[0] + jnp.log2(roww[1])
    rx1[dp] = roww[1]
    to_all_dp(rx1, 0)
    from_all_dp(rx1, 0)
    lse1 = lse_of(rx1)
    g = exp2(roww[0] - lse1)
    row1 = -math.log2(NN) - lse1
    roww[0] = g

    def col_sums(buf, stage, i, u):
        roww[1] = u
        q = jnp.dot(stacked(row_of(roww.at[1], 8)), e_ref[...], preferred_element_type=F32)
        dense_into(colw, q[0:1, :] + q[1:2, :], 16)
        stage[...] = colw[...]
        buf[noise] = stage[...].astype(BF)
        to_all_noise(buf, i)
        pending.append((buf.at[pl.ds(0, NZ * NY - 1)], csend.at[i]))

    def row_sums(v, buf, i):
        colw[...] = v
        q = lax.dot_general(stacked(row_of(colw, 16)), e_ref[...], (((1,), (1,)), ((), ())), preferred_element_type=F32)
        dense_into(roww.at[1], q[0:1, :] + q[1:2, :], 8)
        buf[dp] = roww[1] * roww[0]
        to_all_dp(buf, i)

    col_sums(cx2, cs2, 1, g)
    spread(roww.at[0], g_b)
    norms = jnp.zeros((1, COLS), F32)
    def col_norm(i, carry):
        v = yt[pl.ds(pl.multiple_of(i * 32, 32), 32), :].astype(F32)
        return carry + jnp.sum((v * v).reshape(4, 8, COLS), axis=0)
    norms = jnp.sum(lax.fori_loop(0, D // 32, col_norm, jnp.zeros((8, COLS), F32)), axis=0, keepdims=True)
    dense_into(cs3, norms, 16)
    from_all_noise(cx2, 1)
    row_sums(1.0 / jnp.sum(cx2[...].astype(F32), axis=0), rx2, 1)
    from_all_dp(rx2, 1)
    t2 = jnp.sum(rx2[...], axis=0)

    col_sums(cx3, cs2, 2, roww[0] / t2)
    from_all_noise(cx3, 2)
    q3 = jnp.sum(cx3[...].astype(F32), axis=0)
    v3 = 1.0 / q3
    col_out[...] = (EPSILON / LOG2E) * (col1 + 2.0 - jnp.log2(q3) + NORM_SCALE * cs3[...])
    colw[...] = v3
    v_row = row_of(colw, 16)

    half = pl.ds(0, ROWS // 2), pl.ds(ROWS // 2, ROWS // 2)
    right, left = dev(z, y, lax.rem(x + 1, NX), c), dev(z, y, lax.rem(x + NX - 1, NX), c)

    def rcopy(src, dst, i, to):
        return pltpu.make_async_remote_copy(
            src_ref=src, dst_ref=dst, send_sem=fsend.at[i], recv_sem=frecv.at[i],
            device_id=to, device_id_type=pl.DeviceIdType.MESH)

    def sib_copy(k, h):
        return pltpu.make_async_remote_copy(
            src_ref=sib_s.at[k, half[h]], dst_ref=sib_r.at[k, half[h]], send_sem=psend.at[2 * k + h], recv_sem=precv.at[2 * k + h],
            device_id=dev(z, y, x, 1 - c), device_id_type=MESH)

    def weigh(k, h):
        first = lax.rem(x + 2 + 3 * k + 3 * (k // 2) + 2 * (k // 3), NX) * 256

        @pl.when(h == 0)
        def _():
            def body(i, carry):
                rows = pl.ds(pl.multiple_of(first + i * 32, 32), 32)
                vy[rows, :] = (yt[rows, :].astype(F32) * v_row).astype(BF)
                return carry

            lax.fori_loop(0, 8, body, 0)

        w = vy[pl.ds(pl.multiple_of(first, 256), 256), :]
        rows = pl.ds(pl.multiple_of(h * (ROWS // 2), ROWS // 2), ROWS // 2)
        p = lax.dot_general(e_ref[rows, :], w, (((1,), (1,)), ((), ())), preferred_element_type=F32)
        gg = g_b[rows, :]
        lo, hi = p[:, :128] * gg, p[:, 128:] * gg
        acc[k, rows, :] = jnp.where(c == 0, lo, hi)
        sib_s[k, rows, :] = jnp.where(c == 0, hi, lo).astype(BF)

    def presum(k, h):
        sib_copy(k, h).wait_recv()
        return acc[k, half[h], :] + sib_r[k, half[h], :].astype(F32)

    far = [rcopy(far_s.at[half[0]], far_r.at[0], 0, right), rcopy(far_s.at[half[1]], far_r.at[1], 1, left)]
    near0 = rcopy(near_s.at[0], near_r.at[0], 2, right)
    near1 = rcopy(near_s.at[1], near_r.at[1], 3, left)
    mrg0 = rcopy(mrg_s.at[0], mrg_r.at[0], 4, right)
    mrg1 = rcopy(mrg_s.at[1], mrg_r.at[1], 5, left)
    def far_go(h):
        far_s[half[h], :] = presum(0, h).astype(BF)
        far[h].start()

    def near0_go():
        near_s[0] = presum(1, 1).astype(BF)
        near0.start()

    def near1_go():
        near_s[1] = presum(2, 0).astype(BF)
        near1.start()

    after = {2: lambda: far_go(0), 3: lambda: far_go(1), 4: near0_go, 5: near1_go}

    def weigh_body(i, carry):
        weigh(i // 2, i % 2)
        for j in range(8):
            @pl.when(i == j)
            def _():
                sib_copy(j // 2, j % 2).start()
                if j in after:
                    after[j]()
        return carry

    lax.fori_loop(0, 8, weigh_body, 0)
    row_sums(v3, rx3, 2)
    far[0].wait_recv()
    mrg_s[0] = (presum(1, 0) + far_r[0].astype(F32)).astype(BF)
    mrg0.start()
    far[1].wait_recv()
    mrg_s[1] = (presum(2, 1) + far_r[1].astype(F32)).astype(BF)
    mrg1.start()
    acc[3, half[0], :] = presum(3, 0)
    acc[3, half[1], :] = presum(3, 1)
    from_all_dp(rx3, 2)
    t3 = jnp.sum(rx3[...], axis=0)
    row_out[...] = (EPSILON / LOG2E) * (row1 - 2.0 - jnp.log2(t3))
    roww[1] = 1.0 / t3
    spread(roww.at[1], t_b)
    near0.wait_recv()
    near1.wait_recv()
    mrg0.wait_recv()
    tgt_out[half[0], :] = ((acc[3, half[0], :] + near_r[1].astype(F32) + mrg_r[0].astype(F32)) * t_b[half[0], :]).astype(BF)
    mrg1.wait_recv()
    tgt_out[half[1], :] = ((acc[3, half[1], :] + near_r[0].astype(F32) + mrg_r[1].astype(F32)) * t_b[half[1], :]).astype(BF)

    for d in far + [near0, near1, mrg0, mrg1]:
        d.wait_send()
    for k in range(4):
        for h in range(2):
            sib_copy(k, h).wait_send()
    finish()


def place(row_in, col_in, tgt_in, row_out, col_out, tgt_out):
    row_out[...] = row_in[...]
    col_out[...] = col_in[...]
    tgt_out[...] = tgt_in[...]


def local(noise_batch, latents):
    v = pltpu.VMEM
    dma = pltpu.SemaphoreType.DMA
    row, col, tgt = pl.pallas_call(
        kernel,
        out_shape=(
            jax.ShapeDtypeStruct((8, 128), F32),
            jax.ShapeDtypeStruct((16, 128), F32),
            jax.ShapeDtypeStruct((ROWS, 128), BF),
        ),
        in_specs=[pl.BlockSpec(memory_space=pl.ANY)] * 2,
        out_specs=[pl.BlockSpec(memory_space=pltpu.VMEM)] * 3,
        scratch_shapes=[
            v((D, COLS), BF),
            v((ROWS, D), BF),
            v((ROWS, COLS), F32),
            v((ROWS, COLS), BF),
            v((D, COLS), BF),
            v((ROWS, 128), F32),
            v((ROWS, 128), F32),
            v((ROWS, 128), F32),
            v((ROWS, 128), F32),
            v((ROWS, 128), F32),
            v((16, 128), F32),
            v((2, 8, 128), F32),
            v((32, 8, 128), F32),
            v((32, 16, 128), BF),
            v((32, 16, 128), BF),
            v((32, 8, 128), F32),
            v((16, 128), F32),
            v((16, 128), F32),
            v((8, 8, 128), F32),
            v((8, 8, 128), F32),
            v((8, 8, 128), F32),
            v((4, ROWS, 128), BF),
            v((4, ROWS, 128), BF),
            v((4, ROWS, 128), F32),
            v((ROWS, 128), BF),
            v((2, ROWS // 2, 128), BF),
            v((2, ROWS // 2, 128), BF),
            v((2, ROWS // 2, 128), BF),
            v((2, ROWS // 2, 128), BF),
            v((2, ROWS // 2, 128), BF),
            dma((2,)),
            dma,
            dma((len(KEYS),)),
            dma((len(XKEYS),)),
            dma((len(XKEYS),)),
            dma((4,)),
            dma((4,)),
            dma((3,)),
            dma((3,)),
            dma((8,)),
            dma((8,)),
            dma((6,)),
            dma((6,)),
        ],
        compiler_params=pltpu.CompilerParams(
            collective_id=0, has_side_effects=True, vmem_limit_bytes=56 * 2**20),
        cost_estimate=pl.CostEstimate(flops=4 * ROWS * COLS * D, bytes_accessed=2**20, transcendentals=2 * ROWS * COLS),
    )(noise_batch, latents.T)
    row, col, tgt = pl.pallas_call(
        place,
        out_shape=(
            jax.ShapeDtypeStruct((8, 128), F32),
            jax.ShapeDtypeStruct((16, 128), F32),
            jax.ShapeDtypeStruct((ROWS, 128), BF),
        ),
        in_specs=[pl.BlockSpec(memory_space=pltpu.VMEM)] * 3,
        out_specs=[pl.BlockSpec(memory_space=pltpu.VMEM)] * 3,
        compiler_params=pltpu.CompilerParams(vmem_limit_bytes=60 * 2**20),
    )(row, col, tgt)
    return row.reshape(ROWS), col.reshape(COLS), tgt


def solution(mesh):
    in_specs = (P("noise", "dp"), P("dp", "noise"))
    out_specs = (P("noise"), P("dp"), P("noise", "dp"))
    return jax.shard_map(local, mesh=mesh, in_specs=in_specs, out_specs=out_specs, check_vma=False)
```

```python
import math

import jax
import jax.numpy as jnp
from jax import lax
from jax.experimental import pallas as pl
from jax.experimental.pallas import tpu as pltpu
from jax.sharding import PartitionSpec as P

EPSILON = 0.01
NZ, NY, NX, NC = 8, 4, 4, 2
ROWS, COLS, D = 1024, 2048, 1024
NN, NM = 32768, 16384
LOG2E = math.log2(math.e)
NORM_SCALE = LOG2E / (EPSILON * D)
CROSS_SCALE = 2.0 * NORM_SCALE
STRIP = 256

BF = jnp.bfloat16
F32 = jnp.float32

HELD_AT = {
    'Az': {('p', 1): 0, ('p', 2): 1, ('p', 3): 2, ('p', 4): 3, ('q', 1): 0, ('q', 2): 1, ('q', 3): 2},
    'By': {('p', 1): 0, ('q', 1): 0, ('p', 2): 1},
    'Ay': {('p', 1): 0, ('q', 1): 0, ('p', 2): 1},
    'Bz': {('p', 1): 0, ('p', 2): 1, ('p', 3): 2, ('p', 4): 3, ('q', 1): 0, ('q', 2): 1, ('q', 3): 2},
}
GROUPS = (('A', 0, 768), ('B', 768, 256), ('A', 1024, 512), ('B', 1536, 512))
GATHER = (
    ('go', 0), ('go', 1), ('go', 2), ('go', 3), ('XS', 0), ('Az', 0, 'p', 1), ('Az', 0, 'q', 1), ('Ay', 0, 'p', 1, 0),
    ('Ay', 0, 'q', 1, 0), ('Bz', 1, 'p', 1, 0), ('Bz', 1, 'q', 1, 0), ('By', 1, 'p', 1), ('By', 1, 'q', 1),
    ('Az', 2, 'p', 1), ('Az', 2, 'q', 1), ('Ay', 2, 'p', 1, 0), ('Ay', 2, 'q', 1, 0), ('Bz', 3, 'p', 1, 0),
    ('Bz', 3, 'q', 1, 0), ('By', 3, 'p', 1), ('By', 3, 'q', 1), ('Az', 0, 'p', 2), ('Ay', 0, 'p', 1, -1),
    ('Ay', 0, 'q', 1, -1), ('Az', 0, 'q', 2), ('Ay', 0, 'p', 1, 1), ('Ay', 0, 'q', 1, 1), ('Bz', 1, 'p', 2, 0),
    ('Bz', 1, 'q', 2, 0), ('Bz', 1, 'p', 1, -1), ('X', 'p', 1), ('Bz', 1, 'q', 1, -1), ('X', 'q', 1),
    ('Bz', 1, 'p', 1, 1), ('Ay', 0, 'p', 2, 0), ('Bz', 1, 'q', 1, 1), ('Az', 2, 'p', 2), ('Az', 2, 'q', 2),
    ('By', 1, 'p', 2), ('XS', 1), ('Bz', 3, 'p', 2, 0), ('Ay', 2, 'p', 1, -1), ('XS', 2), ('Ay', 2, 'q', 1, -1),
    ('Bz', 3, 'q', 2, 0), ('Bz', 3, 'p', 1, -1), ('Ay', 2, 'p', 1, 1), ('Ay', 2, 'q', 1, 1), ('Bz', 3, 'q', 1, -1),
    ('Bz', 3, 'p', 1, 1), ('Ay', 2, 'p', 2, 0), ('Bz', 3, 'q', 1, 1), ('By', 3, 'p', 2), ('Az', 0, 'p', 3),
    ('Ay', 0, 'p', 1, -2), ('Ay', 0, 'q', 1, -2), ('Az', 0, 'q', 3), ('Ay', 0, 'p', 2, -1), ('Ay', 0, 'q', 1, 2),
    ('Bz', 1, 'p', 3, 0), ('Bz', 1, 'q', 3, 0), ('Bz', 1, 'p', 2, -1), ('Bz', 1, 'q', 2, -1), ('Bz', 1, 'p', 2, 1),
    ('Ay', 0, 'p', 1, 2), ('Bz', 1, 'q', 2, 1), ('Az', 2, 'p', 3), ('Az', 2, 'q', 3), ('Ay', 0, 'p', 2, 1),
    ('Bz', 1, 'q', 1, 2), ('X', 'p', 2), ('Bz', 1, 'p', 1, 2), ('Bz', 3, 'p', 3, 0), ('Ay', 2, 'p', 1, -2),
    ('Ay', 2, 'q', 1, -2), ('Bz', 3, 'q', 3, 0), ('Bz', 3, 'p', 2, -1), ('Ay', 2, 'p', 1, 2), ('Ay', 2, 'q', 1, 2),
    ('Bz', 3, 'q', 2, -1), ('Bz', 3, 'p', 2, 1), ('Bz', 3, 'q', 2, 1), ('XS', 3), ('norm',), ('Ay', 2, 'p', 2, -1),
    ('Ay', 2, 'p', 2, 1), ('Bz', 3, 'q', 1, 2), ('Bz', 3, 'p', 1, 2), ('Ay', 0, 'p', 1, -3), ('Ay', 0, 'q', 1, -3),
    ('Ay', 0, 'p', 2, -2), ('Ay', 0, 'q', 1, 3), ('Az', 0, 'p', 4), ('Bz', 1, 'p', 4, 0), ('Bz', 1, 'q', 3, -1),
    ('Bz', 1, 'p', 3, -1), ('Ay', 0, 'p', 1, 3), ('Bz', 1, 'q', 3, 1), ('Bz', 1, 'p', 3, 1), ('Bz', 1, 'q', 2, 2),
    ('Az', 2, 'p', 4), ('Bz', 1, 'p', 2, 2), ('dot', 0, 0), ('Bz', 3, 'p', 4, 0), ('dot', 0, 1), ('Ay', 0, 'p', 2, 2),
    ('Bz', 3, 'q', 3, -1), ('Bz', 3, 'p', 3, -1), ('Ay', 2, 'p', 1, -3), ('Ay', 2, 'q', 1, -3), ('dot', 0, 2),
    ('Bz', 3, 'q', 3, 1), ('Bz', 3, 'p', 3, 1), ('Ay', 2, 'p', 1, 3), ('Ay', 2, 'q', 1, 3), ('Bz', 3, 'q', 2, 2),
    ('dot', 0, 3), ('Bz', 3, 'p', 2, 2), ('Ay', 2, 'p', 2, -2), ('Ay', 2, 'p', 2, 2), ('dot', 0, 4),
    ('Bz', 1, 'p', 4, -1), ('Bz', 1, 'p', 4, 1), ('Bz', 1, 'p', 3, 2), ('dot', 0, 5), ('Ay', 0, 'p', 2, -3),
    ('Ay', 0, 'q', 1, -4), ('Bz', 1, 'q', 3, 2), ('Ay', 0, 'p', 1, -4), ('dot', 0, 6), ('Bz', 3, 'p', 4, -1),
    ('Bz', 3, 'p', 4, 1), ('Ay', 0, 'p', 2, 3), ('dot', 0, 7), ('Bz', 3, 'q', 3, 2), ('Ay', 2, 'p', 1, -4),
    ('Bz', 3, 'p', 3, 2), ('Ay', 2, 'q', 1, -4), ('Ay', 2, 'p', 2, -3), ('Bz', 1, 'p', 4, 2), ('Ay', 2, 'p', 2, 3),
    ('Ay', 0, 'p', 2, -4), ('dot', 1, 0), ('Ay', 2, 'p', 2, -4), ('dot', 1, 1), ('Bz', 3, 'p', 4, 2), ('dot', 1, 2),
    ('dot', 1, 3), ('dot', 1, 4), ('dot', 1, 5), ('dot', 1, 6), ('dot', 1, 7),
)
DEPTHS = ((0, -1, 1, -2), (2, -3, 3, -4))
KEYS = [e for e in GATHER if e[0] in ("Az", "Ay", "By", "Bz")]
assert len(set(KEYS)) == len(KEYS) == 31 * len(GROUPS)
SEM_OF = {k: i for i, k in enumerate(KEYS)}
XKEYS = [("X", "p", 1), ("X", "q", 1), ("X", "p", 2), ("XS", 0), ("XS", 1), ("XS", 2), ("XS", 3)]
XSEM_OF = {k: i for i, k in enumerate(XKEYS)}

FAR_FIRST = sorted(
    ((dz, dy) for dz in range(-3, 5) for dy in range(-1, 3) if dz or dy),
    key=lambda p: (-abs(p[0]) - abs(p[1]), p))


def exp2(v):
    return jnp.exp2(v)


def kernel(noise_ref, lat_ref, row_out, col_out, tgt_out,
           yt, xb, s_ref, e_ref, vy, sq, m_b, l_b, g_b, t_b, colw, roww,
           cx1, cx2, cx3, cx4, cs2, cs3, rx1, rx2, rx3,
           sib_s, sib_r, acc, far_s, far_r, near_s, near_r, mrg_s, mrg_r,
           in_sem, ysend, yrecv, xsend, xrecv, csend, crecv, rsend, rrecv, psend, precv, fsend, frecv):
    noise = lax.axis_index("noise")
    dp = lax.axis_index("dp")
    z, y = noise // NY, noise % NY
    x, c = dp // NC, dp % NC
    s = 1 - 2 * c

    def dev(zz, yy, xx, cc):
        return {"noise": zz * NY + yy, "dp": xx * NC + cc}

    def zat(k):
        return lax.rem(z + s * k + 2 * NZ, NZ)

    def yat(k):
        return lax.rem(y + s * k + 2 * NY, NY)

    def xat(k):
        return lax.rem(x + s * k + 2 * NX, NX)

    def yrow(zz, yy):
        return pl.multiple_of(zz * 128 + yy * 32, 32)

    own_x = pl.multiple_of(dp * 128, 128)
    load_lat = pltpu.make_async_copy(lat_ref, yt.at[pl.ds(yrow(z, y), 32), :], in_sem.at[0])
    load_x = pltpu.make_async_copy(noise_ref, xb.at[:, pl.ds(own_x, 128)], in_sem.at[1])
    load_lat.start()
    load_x.start()

    MESH = pl.DeviceIdType.MESH
    barrier = pltpu.get_barrier_semaphore()
    around = [dev(zat(1), y, x, c), dev(zat(-1), y, x, c), dev(z, yat(1), x, c), dev(z, yat(-1), x, c),
              dev(z, y, xat(1), c), dev(z, y, xat(-1), c), dev(z, y, x, 1 - c)]
    for to in around:
        pl.semaphore_signal(barrier, 1, device_id=to, device_id_type=MESH)

    load_lat.wait()
    load_x.wait()
    pl.semaphore_wait(barrier, len(around))

    pending = []

    def finish():
        for part, sem in pending:
            pltpu.make_async_copy(part, part, sem).wait()

    def xblk(xx, cc):
        return xb.at[:, pl.ds(pl.multiple_of((xx * NC + cc) * 128, 128), 128)]

    def sgn(pq):
        return 1 if pq == "p" else -1

    def block(key, dist):
        kind, g, o = key[0], key[1], sgn(key[2])
        if kind == "Az":
            at = zat(-o * dist), y
        elif kind == "Ay":
            at = zat(key[4]), yat(-o * dist)
        elif kind == "By":
            at = z, yat(-o * dist)
        else:
            at = zat(-o * dist), yat(key[4])
        return yt.at[pl.ds(yrow(*at), 32), pl.ds(GROUPS[g][1], GROUPS[g][2])]

    def desc(key):
        kind = key[0]
        if kind == "X":
            o = sgn(key[1])
            blk = xblk(xat(-o * (key[2] - 1)), c)
            to = dev(z, y, xat(o), c)
            sems = xsend, xrecv, XSEM_OF[key]
        elif kind == "XS":
            blk = xblk(xat((0, -1, 1, -2)[key[1]]), c)
            to = dev(z, y, x, 1 - c)
            sems = xsend, xrecv, XSEM_OF[key]
        else:
            o = sgn(key[2])
            held = HELD_AT[kind][key[2:4]]
            blk = block(key, held)
            step = o * (key[3] - held)
            to = dev(zat(step), y, x, c) if kind[1] == "z" else dev(z, yat(step), x, c)
            return pltpu.make_async_remote_copy(
                src_ref=blk, dst_ref=blk, send_sem=ysend, recv_sem=yrecv.at[SEM_OF[key]],
                device_id=to, device_id_type=MESH)
        i = sems[2]
        return pltpu.make_async_remote_copy(
            src_ref=blk, dst_ref=blk, send_sem=sems[0].at[i], recv_sem=sems[1].at[i],
            device_id=to, device_id_type=pl.DeviceIdType.MESH)

    def arrive(key):
        kind = key[0]
        if kind == "X":
            blk = xblk(xat(-sgn(key[1]) * key[2]), c)
            sem = xrecv.at[XSEM_OF[key]]
        elif kind == "XS":
            blk = xblk(xat((0, 1, -1, 2)[key[1]]), 1 - c)
            sem = xrecv.at[XSEM_OF[key]]
        else:
            blk = block(key, key[3])
            sem = yrecv.at[SEM_OF[key]]
        pltpu.make_async_copy(blk, blk, sem).wait()

    def add_squares(blk_ref, first):
        v = blk_ref[...].astype(F32)
        sq[...] = v * v if first else sq[...] + v * v

    def dot_strip(half, strip):
        cols = pl.ds(pl.multiple_of(strip * STRIP, STRIP), STRIP)
        rows = [pl.ds(pl.multiple_of(zat(k) * 128, 128), 128) for k in DEPTHS[half]]
        lhs = jnp.concatenate([xb[:, r] for r in rows], axis=1)
        rhs = jnp.concatenate([yt[r, cols] for r in rows], axis=0)
        v = CROSS_SCALE * jnp.dot(lhs, rhs, preferred_element_type=F32)
        if half == 0:
            a = m_b[...]
            s_ref[:, cols] = v + jnp.concatenate([a, a], axis=1)
            return
        v = s_ref[:, cols] + v
        s_ref[:, cols] = v
        peak = jnp.max(jnp.max(v.reshape(ROWS // 8, 8, STRIP), axis=0), axis=0, keepdims=True)
        total = jnp.zeros((8, STRIP), F32)
        for r in range(0, ROWS, 256):
            e = exp2(s_ref[r:r + 256, cols] - peak)
            total = total + jnp.sum(e.reshape(32, 8, STRIP), axis=0)
        lse = peak + jnp.log2(jnp.sum(total, axis=0, keepdims=True))
        for h in range(STRIP // 128):
            colw[pl.ds(strip * (STRIP // 128) + h, 1), :] = lse[:, h * 128:(h + 1) * 128]

    def dense_into(ref, row, n):
        for k in range(n):
            ref[k:k + 1, :] = row[:, k * 128:(k + 1) * 128]

    def to_all_noise(buf, i):
        for dz, dy in FAR_FIRST:
            pltpu.make_async_remote_copy(
                src_ref=buf.at[noise], dst_ref=buf.at[noise], send_sem=csend.at[i], recv_sem=crecv.at[i],
                device_id=dev(zat(dz), yat(dy), x, c), device_id_type=MESH).start()

    def from_all_noise(buf, i):
        part = buf.at[pl.ds(0, NZ * NY - 1)]
        pltpu.make_async_copy(part, part, crecv.at[i]).wait()

    desc(("X", "p", 1)).start()
    desc(("X", "q", 1)).start()
    desc(("XS", 0)).start()
    add_squares(xblk(x, c), True)

    def send_on(kind, g, held, slot=(), only="pq"):
        for o in only:
            for (direction, dist), at in HELD_AT[kind].items():
                if direction == o and at == held:
                    desc((kind, g, o, dist) + slot).start()

    def handle(key):
        kind = key[0]
        if kind == "norm":
            m_b[...] = jnp.broadcast_to(-NORM_SCALE * jnp.sum(sq[...], axis=1, keepdims=True), (ROWS, 128))
            return
        if kind == "go":
            g = key[1]
            near, far = ("Az", "Ay") if GROUPS[g][0] == "A" else ("By", "Bz")
            send_on(near, g, 0)
            send_on(far, g, 0, (0,))
            return
        arrive(key)
        if kind in ("Az", "By"):
            g, pq, d = key[1:]
            send_on(kind, g, d, only=pq)
            if kind == "Az":
                send_on("Ay", g, 0, (-sgn(pq) * d,))
            else:
                send_on("Bz", g, 0, (2 if d == 2 else -sgn(pq),))
        elif kind in ("Ay", "Bz"):
            g, pq, d, slot = key[1:]
            send_on(kind, g, d, (slot,), only=pq)
        elif kind == "X":
            if key == ("X", "p", 1):
                desc(("X", "p", 2)).start()
            desc(("XS", {("p", 1): 1, ("q", 1): 2, ("p", 2): 3}[key[1:]])).start()
            add_squares(xblk(xat(-sgn(key[1]) * key[2]), c), False)
        elif kind == "XS":
            add_squares(xblk(xat((0, 1, -1, 2)[key[1]]), 1 - c), False)

    ahead, steps_now = [], []
    for key in GATHER:
        if key[0] == "dot":
            ahead.append((key[1:], steps_now))
            steps_now = []
        else:
            steps_now.append(key)
    strips = COLS // STRIP
    assert [k for k, _ in ahead] == [(h, i) for h in range(2) for i in range(strips)] and not steps_now

    for half_no in range(2):
        def strip_body(i, carry, half_no=half_no):
            for j in range(strips):
                todo = ahead[half_no * strips + j][1]
                if todo and (half_no, j) != (0, 0):
                    @pl.when(i == j)
                    def _():
                        for key in todo:
                            handle(key)
            if half_no:
                @pl.when(i == strips // 2)
                def _():
                    cx1[noise] = colw[0:8, :]
                    to_all_noise(cx1, 0)
            dot_strip(half_no, i)
            return carry

        if half_no == 0:
            for key in ahead[0][1]:
                handle(key)
        lax.fori_loop(0, strips, strip_body, 0)
    cx4[noise] = colw[8:16, :]
    to_all_noise(cx4, 3)
    pending.append((cx1.at[pl.ds(0, NZ * NY - 1)], csend.at[0]))
    pending.append((cx4.at[pl.ds(0, NZ * NY - 1)], csend.at[3]))
    pending.append((yt.at[pl.ds(0, (NZ * NY - 1) * 32), pl.ds(0, sum(g[2] for g in GROUPS))], ysend))
    for i in range(len(XKEYS)):
        pending.append((xblk(x, c), xsend.at[i]))

    def to_all_dp(buf, i):
        for dx, dc in ((2, 0), (2, 1), (1, 0), (1, 1), (-1, 0), (-1, 1), (0, 1)):
            pltpu.make_async_remote_copy(
                src_ref=buf.at[dp], dst_ref=buf.at[dp], send_sem=rsend.at[i], recv_sem=rrecv.at[i],
                device_id=dev(z, y, xat(dx), 1 - c if dc else c), device_id_type=MESH).start()
        pending.append((buf.at[pl.ds(0, NX * NC - 1)], rsend.at[i]))

    def from_all_dp(buf, i):
        part = buf.at[pl.ds(0, NX * NC - 1)]
        pltpu.make_async_copy(part, part, rrecv.at[i]).wait()

    def row_of(ref, n):
        return jnp.concatenate([ref[k:k + 1, :] for k in range(n)], axis=1)

    def stacked(row):
        n = row.shape[1]
        hi = row.astype(BF).astype(F32)
        lo = row - hi
        i = lax.broadcasted_iota(jnp.int32, (16, n), 0)
        return jnp.where(i == 0, jnp.broadcast_to(hi, (16, n)), jnp.where(i == 1, jnp.broadcast_to(lo, (16, n)), 0.0)).astype(BF)

    def lse_of(buf):
        v = buf[...]
        peak = jnp.max(v, axis=0)
        return peak + jnp.log2(jnp.sum(exp2(v - peak[None]), axis=0))

    def spread(ref, out):
        for b in range(ROWS // 128):
            out[b * 128:(b + 1) * 128, :] = jnp.broadcast_to(ref[b:b + 1, :], (128, 128)).T

    from_all_noise(cx1, 0)
    lse_a = lse_of(cx1)
    from_all_noise(cx4, 3)
    lse_b = lse_of(cx4)
    colw[0:8, :] = lse_a
    colw[8:16, :] = lse_b
    col1 = -math.log2(NM) - colw[...]
    colw[...] = col1

    col_row = row_of(colw, 16)

    def lane_tiles(v):
        return [v[:, k * 128:(k + 1) * 128] for k in range(COLS // 128)]

    def tree(op, parts):
        while len(parts) > 1:
            parts = [op(*parts[i:i + 2]) for i in range(0, len(parts), 2)]
        return parts[0]

    def row_peaks(i, carry):
        rows = pl.ds(pl.multiple_of(i * 16, 16), 16)
        l_b[rows, :] = tree(jnp.maximum, lane_tiles(s_ref[rows, :] + col_row))
        return carry

    lax.fori_loop(0, ROWS // 16, row_peaks, 0, unroll=4)
    for b in range(ROWS // 128):
        blk = pl.ds(b * 128, 128)
        t = l_b[blk, :]
        m_b[blk, :] = jnp.broadcast_to(jnp.max(t, axis=1, keepdims=True), (128, 128))
        roww[0, b:b + 1, :] = jnp.max(t.T, axis=0, keepdims=True)

    def row_exps(i, carry):
        rows = pl.ds(pl.multiple_of(i * 16, 16), 16)
        peak = m_b[rows, :]
        parts = [exp2(v - peak) for v in lane_tiles(s_ref[rows, :] + col_row)]
        for k, e in enumerate(parts):
            e_ref[rows, k * 128:(k + 1) * 128] = e.astype(BF)
        l_b[rows, :] = tree(jnp.add, parts)
        return carry

    lax.fori_loop(0, ROWS // 16, row_exps, 0, unroll=4)
    for b in range(ROWS // 128):
        t = l_b[b * 128:(b + 1) * 128, :].T
        roww[1, b:b + 1, :] = jnp.sum(t, axis=0, keepdims=True)
    roww[1] = roww[0] + jnp.log2(roww[1])
    rx1[dp] = roww[1]
    to_all_dp(rx1, 0)
    from_all_dp(rx1, 0)
    lse1 = lse_of(rx1)
    g = exp2(roww[0] - lse1)
    row1 = -math.log2(NN) - lse1
    roww[0] = g

    def col_sums(buf, stage, i, u):
        roww[1] = u
        q = jnp.dot(stacked(row_of(roww.at[1], 8)), e_ref[...], preferred_element_type=F32)
        dense_into(colw, q[0:1, :] + q[1:2, :], 16)
        stage[...] = colw[...]
        buf[noise] = stage[...].astype(BF)
        to_all_noise(buf, i)
        pending.append((buf.at[pl.ds(0, NZ * NY - 1)], csend.at[i]))

    def row_sums(v, buf, i):
        colw[...] = v
        q = lax.dot_general(stacked(row_of(colw, 16)), e_ref[...], (((1,), (1,)), ((), ())), preferred_element_type=F32)
        dense_into(roww.at[1], q[0:1, :] + q[1:2, :], 8)
        buf[dp] = roww[1] * roww[0]
        to_all_dp(buf, i)

    col_sums(cx2, cs2, 1, g)
    spread(roww.at[0], g_b)
    norms = jnp.zeros((1, COLS), F32)
    def col_norm(i, carry):
        v = yt[pl.ds(pl.multiple_of(i * 32, 32), 32), :].astype(F32)
        return carry + jnp.sum((v * v).reshape(4, 8, COLS), axis=0)
    norms = jnp.sum(lax.fori_loop(0, D // 32, col_norm, jnp.zeros((8, COLS), F32)), axis=0, keepdims=True)
    dense_into(cs3, norms, 16)
    from_all_noise(cx2, 1)
    row_sums(1.0 / jnp.sum(cx2[...].astype(F32), axis=0), rx2, 1)
    from_all_dp(rx2, 1)
    t2 = jnp.sum(rx2[...], axis=0)

    col_sums(cx3, cs2, 2, roww[0] / t2)
    from_all_noise(cx3, 2)
    q3 = jnp.sum(cx3[...].astype(F32), axis=0)
    v3 = 1.0 / q3
    col_out[...] = (EPSILON / LOG2E) * (col1 + 2.0 - jnp.log2(q3) + NORM_SCALE * cs3[...])
    colw[...] = v3
    v_row = row_of(colw, 16)

    half = pl.ds(0, ROWS // 2), pl.ds(ROWS // 2, ROWS // 2)
    right, left = dev(z, y, lax.rem(x + 1, NX), c), dev(z, y, lax.rem(x + NX - 1, NX), c)

    def rcopy(src, dst, i, to):
        return pltpu.make_async_remote_copy(
            src_ref=src, dst_ref=dst, send_sem=fsend.at[i], recv_sem=frecv.at[i],
            device_id=to, device_id_type=pl.DeviceIdType.MESH)

    def sib_copy(k, h):
        return pltpu.make_async_remote_copy(
            src_ref=sib_s.at[k, half[h]], dst_ref=sib_r.at[k, half[h]], send_sem=psend.at[2 * k + h], recv_sem=precv.at[2 * k + h],
            device_id=dev(z, y, x, 1 - c), device_id_type=MESH)

    def weigh(k, h):
        first = lax.rem(x + 2 + 3 * k + 3 * (k // 2) + 2 * (k // 3), NX) * 256

        @pl.when(h == 0)
        def _():
            def body(i, carry):
                rows = pl.ds(pl.multiple_of(first + i * 32, 32), 32)
                vy[rows, :] = (yt[rows, :].astype(F32) * v_row).astype(BF)
                return carry

            lax.fori_loop(0, 8, body, 0)

        w = vy[pl.ds(pl.multiple_of(first, 256), 256), :]
        rows = pl.ds(pl.multiple_of(h * (ROWS // 2), ROWS // 2), ROWS // 2)
        p = lax.dot_general(e_ref[rows, :], w, (((1,), (1,)), ((), ())), preferred_element_type=F32)
        gg = g_b[rows, :]
        lo, hi = p[:, :128] * gg, p[:, 128:] * gg
        acc[k, rows, :] = jnp.where(c == 0, lo, hi)
        sib_s[k, rows, :] = jnp.where(c == 0, hi, lo).astype(BF)

    def presum(k, h):
        sib_copy(k, h).wait_recv()
        return acc[k, half[h], :] + sib_r[k, half[h], :].astype(F32)

    far = [rcopy(far_s.at[half[0]], far_r.at[0], 0, right), rcopy(far_s.at[half[1]], far_r.at[1], 1, left)]
    near0 = rcopy(near_s.at[0], near_r.at[0], 2, right)
    near1 = rcopy(near_s.at[1], near_r.at[1], 3, left)
    mrg0 = rcopy(mrg_s.at[0], mrg_r.at[0], 4, right)
    mrg1 = rcopy(mrg_s.at[1], mrg_r.at[1], 5, left)
    def far_go(h):
        far_s[half[h], :] = presum(0, h).astype(BF)
        far[h].start()

    def near0_go():
        near_s[0] = presum(1, 1).astype(BF)
        near0.start()

    def near1_go():
        near_s[1] = presum(2, 0).astype(BF)
        near1.start()

    after = {2: lambda: far_go(0), 3: lambda: far_go(1), 5: near0_go, 6: near1_go}

    def weigh_body(i, carry):
        weigh(i // 2, i % 2)
        for j in range(8):
            @pl.when(i == j)
            def _():
                sib_copy(j // 2, j % 2).start()
                if j in after:
                    after[j]()
        return carry

    lax.fori_loop(0, 8, weigh_body, 0)
    row_sums(v3, rx3, 2)
    far[0].wait_recv()
    mrg_s[0] = (presum(1, 0) + far_r[0].astype(F32)).astype(BF)
    mrg0.start()
    far[1].wait_recv()
    mrg_s[1] = (presum(2, 1) + far_r[1].astype(F32)).astype(BF)
    mrg1.start()
    acc[3, half[0], :] = presum(3, 0)
    acc[3, half[1], :] = presum(3, 1)
    from_all_dp(rx3, 2)
    t3 = jnp.sum(rx3[...], axis=0)
    row_out[...] = (EPSILON / LOG2E) * (row1 - 2.0 - jnp.log2(t3))
    roww[1] = 1.0 / t3
    spread(roww.at[1], t_b)
    near0.wait_recv()
    near1.wait_recv()
    mrg0.wait_recv()
    tgt_out[half[0], :] = ((acc[3, half[0], :] + near_r[1].astype(F32) + mrg_r[0].astype(F32)) * t_b[half[0], :]).astype(BF)
    mrg1.wait_recv()
    tgt_out[half[1], :] = ((acc[3, half[1], :] + near_r[0].astype(F32) + mrg_r[1].astype(F32)) * t_b[half[1], :]).astype(BF)

    for d in far + [near0, near1, mrg0, mrg1]:
        d.wait_send()
    for k in range(4):
        for h in range(2):
            sib_copy(k, h).wait_send()
    finish()


def place(row_in, col_in, tgt_in, row_out, col_out, tgt_out):
    row_out[...] = row_in[...]
    col_out[...] = col_in[...]
    tgt_out[...] = tgt_in[...]


def local(noise_batch, latents):
    v = pltpu.VMEM
    dma = pltpu.SemaphoreType.DMA
    row, col, tgt = pl.pallas_call(
        kernel,
        out_shape=(
            jax.ShapeDtypeStruct((8, 128), F32),
            jax.ShapeDtypeStruct((16, 128), F32),
            jax.ShapeDtypeStruct((ROWS, 128), BF),
        ),
        in_specs=[pl.BlockSpec(memory_space=pl.ANY)] * 2,
        out_specs=[pl.BlockSpec(memory_space=pltpu.VMEM)] * 3,
        scratch_shapes=[
            v((D, COLS), BF),
            v((ROWS, D), BF),
            v((ROWS, COLS), F32),
            v((ROWS, COLS), BF),
            v((D, COLS), BF),
            v((ROWS, 128), F32),
            v((ROWS, 128), F32),
            v((ROWS, 128), F32),
            v((ROWS, 128), F32),
            v((ROWS, 128), F32),
            v((16, 128), F32),
            v((2, 8, 128), F32),
            v((32, 8, 128), F32),
            v((32, 16, 128), BF),
            v((32, 16, 128), BF),
            v((32, 8, 128), F32),
            v((16, 128), F32),
            v((16, 128), F32),
            v((8, 8, 128), F32),
            v((8, 8, 128), F32),
            v((8, 8, 128), F32),
            v((4, ROWS, 128), BF),
            v((4, ROWS, 128), BF),
            v((4, ROWS, 128), F32),
            v((ROWS, 128), BF),
            v((2, ROWS // 2, 128), BF),
            v((2, ROWS // 2, 128), BF),
            v((2, ROWS // 2, 128), BF),
            v((2, ROWS // 2, 128), BF),
            v((2, ROWS // 2, 128), BF),
            dma((2,)),
            dma,
            dma((len(KEYS),)),
            dma((len(XKEYS),)),
            dma((len(XKEYS),)),
            dma((4,)),
            dma((4,)),
            dma((3,)),
            dma((3,)),
            dma((8,)),
            dma((8,)),
            dma((6,)),
            dma((6,)),
        ],
        compiler_params=pltpu.CompilerParams(
            collective_id=0, has_side_effects=True, vmem_limit_bytes=56 * 2**20),
        cost_estimate=pl.CostEstimate(flops=4 * ROWS * COLS * D, bytes_accessed=2**20, transcendentals=2 * ROWS * COLS),
    )(noise_batch, latents.T)
    row, col, tgt = pl.pallas_call(
        place,
        out_shape=(
            jax.ShapeDtypeStruct((8, 128), F32),
            jax.ShapeDtypeStruct((16, 128), F32),
            jax.ShapeDtypeStruct((ROWS, 128), BF),
        ),
        in_specs=[pl.BlockSpec(memory_space=pltpu.VMEM)] * 3,
        out_specs=[pl.BlockSpec(memory_space=pltpu.VMEM)] * 3,
        compiler_params=pltpu.CompilerParams(vmem_limit_bytes=60 * 2**20),
    )(row, col, tgt)
    return row.reshape(ROWS), col.reshape(COLS), tgt


def solution(mesh):
    in_specs = (P("noise", "dp"), P("dp", "noise"))
    out_specs = (P("noise"), P("dp"), P("noise", "dp"))
    return jax.shard_map(local, mesh=mesh, in_specs=in_specs, out_specs=out_specs, check_vma=False)
```

```python
import math

import jax
import jax.numpy as jnp
from jax import lax
from jax.experimental import pallas as pl
from jax.experimental.pallas import tpu as pltpu
from jax.sharding import PartitionSpec as P

EPSILON = 0.01
NZ, NY, NX, NC = 8, 4, 4, 2
ROWS, COLS, D = 1024, 2048, 1024
NN, NM = 32768, 16384
LOG2E = math.log2(math.e)
NORM_SCALE = LOG2E / (EPSILON * D)
CROSS_SCALE = 2.0 * NORM_SCALE
STRIP = 256

BF = jnp.bfloat16
F32 = jnp.float32

HELD_AT = {
    'Az': {('p', 1): 0, ('p', 2): 1, ('p', 3): 2, ('p', 4): 3, ('q', 1): 0, ('q', 2): 1, ('q', 3): 2},
    'By': {('p', 1): 0, ('q', 1): 0, ('p', 2): 1},
    'Ay': {('p', 1): 0, ('q', 1): 0, ('p', 2): 1},
    'Bz': {('p', 1): 0, ('p', 2): 1, ('p', 3): 2, ('p', 4): 3, ('q', 1): 0, ('q', 2): 1, ('q', 3): 2},
}
GROUPS = (('A', 0, 768), ('B', 768, 256), ('A', 1024, 512), ('B', 1536, 512))
GATHER = (
    ('go', 0), ('go', 1), ('go', 2), ('go', 3), ('XS', 0), ('Az', 0, 'p', 1), ('Az', 0, 'q', 1), ('Ay', 0, 'p', 1, 0),
    ('Ay', 0, 'q', 1, 0), ('Bz', 1, 'p', 1, 0), ('Bz', 1, 'q', 1, 0), ('By', 1, 'p', 1), ('By', 1, 'q', 1),
    ('Az', 2, 'p', 1), ('Az', 2, 'q', 1), ('Ay', 2, 'p', 1, 0), ('Ay', 2, 'q', 1, 0), ('Bz', 3, 'p', 1, 0),
    ('Bz', 3, 'q', 1, 0), ('By', 3, 'p', 1), ('By', 3, 'q', 1), ('Az', 0, 'p', 2), ('Ay', 0, 'p', 1, -1),
    ('Ay', 0, 'q', 1, -1), ('Az', 0, 'q', 2), ('Ay', 0, 'p', 1, 1), ('Ay', 0, 'q', 1, 1), ('Bz', 1, 'p', 2, 0),
    ('Bz', 1, 'q', 2, 0), ('Bz', 1, 'p', 1, -1), ('X', 'p', 1), ('Bz', 1, 'q', 1, -1), ('X', 'q', 1),
    ('Bz', 1, 'p', 1, 1), ('Ay', 0, 'p', 2, 0), ('Bz', 1, 'q', 1, 1), ('Az', 2, 'p', 2), ('Az', 2, 'q', 2),
    ('By', 1, 'p', 2), ('XS', 1), ('Bz', 3, 'p', 2, 0), ('Ay', 2, 'p', 1, -1), ('XS', 2), ('Ay', 2, 'q', 1, -1),
    ('Bz', 3, 'q', 2, 0), ('Bz', 3, 'p', 1, -1), ('Ay', 2, 'p', 1, 1), ('Ay', 2, 'q', 1, 1), ('Bz', 3, 'q', 1, -1),
    ('Bz', 3, 'p', 1, 1), ('Ay', 2, 'p', 2, 0), ('Bz', 3, 'q', 1, 1), ('By', 3, 'p', 2), ('Az', 0, 'p', 3),
    ('Ay', 0, 'p', 1, -2), ('Ay', 0, 'q', 1, -2), ('Az', 0, 'q', 3), ('Ay', 0, 'p', 2, -1), ('Ay', 0, 'q', 1, 2),
    ('Bz', 1, 'p', 3, 0), ('Bz', 1, 'q', 3, 0), ('Bz', 1, 'p', 2, -1), ('Bz', 1, 'q', 2, -1), ('Bz', 1, 'p', 2, 1),
    ('Ay', 0, 'p', 1, 2), ('Bz', 1, 'q', 2, 1), ('Az', 2, 'p', 3), ('Az', 2, 'q', 3), ('Ay', 0, 'p', 2, 1),
    ('Bz', 1, 'q', 1, 2), ('X', 'p', 2), ('Bz', 1, 'p', 1, 2), ('Bz', 3, 'p', 3, 0), ('Ay', 2, 'p', 1, -2),
    ('Ay', 2, 'q', 1, -2), ('Bz', 3, 'q', 3, 0), ('Bz', 3, 'p', 2, -1), ('Ay', 2, 'p', 1, 2), ('Ay', 2, 'q', 1, 2),
    ('Bz', 3, 'q', 2, -1), ('Bz', 3, 'p', 2, 1), ('Bz', 3, 'q', 2, 1), ('XS', 3), ('norm',), ('Ay', 2, 'p', 2, -1),
    ('Ay', 2, 'p', 2, 1), ('Bz', 3, 'q', 1, 2), ('Bz', 3, 'p', 1, 2), ('Ay', 0, 'p', 1, -3), ('Ay', 0, 'q', 1, -3),
    ('Ay', 0, 'p', 2, -2), ('Ay', 0, 'q', 1, 3), ('Az', 0, 'p', 4), ('Bz', 1, 'p', 4, 0), ('Bz', 1, 'q', 3, -1),
    ('Bz', 1, 'p', 3, -1), ('Ay', 0, 'p', 1, 3), ('Bz', 1, 'q', 3, 1), ('Bz', 1, 'p', 3, 1), ('Bz', 1, 'q', 2, 2),
    ('Az', 2, 'p', 4), ('Bz', 1, 'p', 2, 2), ('dot', 0, 0), ('Bz', 3, 'p', 4, 0), ('dot', 0, 1), ('Ay', 0, 'p', 2, 2),
    ('Bz', 3, 'q', 3, -1), ('Bz', 3, 'p', 3, -1), ('Ay', 2, 'p', 1, -3), ('Ay', 2, 'q', 1, -3), ('dot', 0, 2),
    ('Bz', 3, 'q', 3, 1), ('Bz', 3, 'p', 3, 1), ('Ay', 2, 'p', 1, 3), ('Ay', 2, 'q', 1, 3), ('Bz', 3, 'q', 2, 2),
    ('dot', 0, 3), ('Bz', 3, 'p', 2, 2), ('Ay', 2, 'p', 2, -2), ('Ay', 2, 'p', 2, 2), ('dot', 0, 4),
    ('Bz', 1, 'p', 4, -1), ('Bz', 1, 'p', 4, 1), ('Bz', 1, 'p', 3, 2), ('dot', 0, 5), ('Ay', 0, 'p', 2, -3),
    ('Ay', 0, 'q', 1, -4), ('Bz', 1, 'q', 3, 2), ('Ay', 0, 'p', 1, -4), ('dot', 0, 6), ('Bz', 3, 'p', 4, -1),
    ('Bz', 3, 'p', 4, 1), ('Ay', 0, 'p', 2, 3), ('dot', 0, 7), ('Bz', 3, 'q', 3, 2), ('Ay', 2, 'p', 1, -4),
    ('Bz', 3, 'p', 3, 2), ('Ay', 2, 'q', 1, -4), ('Ay', 2, 'p', 2, -3), ('Bz', 1, 'p', 4, 2), ('Ay', 2, 'p', 2, 3),
    ('Ay', 0, 'p', 2, -4), ('dot', 1, 0), ('Ay', 2, 'p', 2, -4), ('dot', 1, 1), ('Bz', 3, 'p', 4, 2), ('dot', 1, 2),
    ('dot', 1, 3), ('dot', 1, 4), ('dot', 1, 5), ('dot', 1, 6), ('dot', 1, 7),
)
DEPTHS = ((0, -1, 1, -2), (2, -3, 3, -4))
KEYS = [e for e in GATHER if e[0] in ("Az", "Ay", "By", "Bz")]
assert len(set(KEYS)) == len(KEYS) == 31 * len(GROUPS)
SEM_OF = {k: i for i, k in enumerate(KEYS)}
XKEYS = [("X", "p", 1), ("X", "q", 1), ("X", "p", 2), ("XS", 0), ("XS", 1), ("XS", 2), ("XS", 3)]
XSEM_OF = {k: i for i, k in enumerate(XKEYS)}

FAR_FIRST = sorted(
    ((dz, dy) for dz in range(-3, 5) for dy in range(-1, 3) if dz or dy),
    key=lambda p: (-abs(p[0]) - abs(p[1]), p))


def exp2(v):
    return jnp.exp2(v)


def kernel(noise_ref, lat_ref, row_out, col_out, tgt_out,
           yt, xb, s_ref, e_ref, vy, sq, m_b, l_b, g_b, t_b, colw, roww,
           cx1, cx2, cx3, cx4, cs2, cs3, rx1, rx2, rx3,
           sib_s, sib_r, acc, far_s, far_r, near_s, near_r, mrg_s, mrg_r,
           in_sem, ysend, yrecv, xsend, xrecv, csend, crecv, rsend, rrecv, psend, precv, fsend, frecv):
    noise = lax.axis_index("noise")
    dp = lax.axis_index("dp")
    z, y = noise // NY, noise % NY
    x, c = dp // NC, dp % NC
    s = 1 - 2 * c

    def dev(zz, yy, xx, cc):
        return {"noise": zz * NY + yy, "dp": xx * NC + cc}

    def zat(k):
        return lax.rem(z + s * k + 2 * NZ, NZ)

    def yat(k):
        return lax.rem(y + s * k + 2 * NY, NY)

    def xat(k):
        return lax.rem(x + s * k + 2 * NX, NX)

    def yrow(zz, yy):
        return pl.multiple_of(zz * 128 + yy * 32, 32)

    own_x = pl.multiple_of(dp * 128, 128)
    load_lat = pltpu.make_async_copy(lat_ref, yt.at[pl.ds(yrow(z, y), 32), :], in_sem.at[0])
    load_x = pltpu.make_async_copy(noise_ref, xb.at[:, pl.ds(own_x, 128)], in_sem.at[1])
    load_lat.start()
    load_x.start()

    MESH = pl.DeviceIdType.MESH
    barrier = pltpu.get_barrier_semaphore()
    around = [dev(zat(1), y, x, c), dev(zat(-1), y, x, c), dev(z, yat(1), x, c), dev(z, yat(-1), x, c),
              dev(z, y, xat(1), c), dev(z, y, xat(-1), c), dev(z, y, x, 1 - c)]
    for to in around:
        pl.semaphore_signal(barrier, 1, device_id=to, device_id_type=MESH)

    load_lat.wait()
    pl.semaphore_wait(barrier, len(around))

    pending = []

    def finish():
        for part, sem in pending:
            pltpu.make_async_copy(part, part, sem).wait()

    def xblk(xx, cc):
        return xb.at[:, pl.ds(pl.multiple_of((xx * NC + cc) * 128, 128), 128)]

    def sgn(pq):
        return 1 if pq == "p" else -1

    def block(key, dist):
        kind, g, o = key[0], key[1], sgn(key[2])
        if kind == "Az":
            at = zat(-o * dist), y
        elif kind == "Ay":
            at = zat(key[4]), yat(-o * dist)
        elif kind == "By":
            at = z, yat(-o * dist)
        else:
            at = zat(-o * dist), yat(key[4])
        return yt.at[pl.ds(yrow(*at), 32), pl.ds(GROUPS[g][1], GROUPS[g][2])]

    def desc(key):
        kind = key[0]
        if kind == "X":
            o = sgn(key[1])
            blk = xblk(xat(-o * (key[2] - 1)), c)
            to = dev(z, y, xat(o), c)
            sems = xsend, xrecv, XSEM_OF[key]
        elif kind == "XS":
            blk = xblk(xat((0, -1, 1, -2)[key[1]]), c)
            to = dev(z, y, x, 1 - c)
            sems = xsend, xrecv, XSEM_OF[key]
        else:
            o = sgn(key[2])
            held = HELD_AT[kind][key[2:4]]
            blk = block(key, held)
            step = o * (key[3] - held)
            to = dev(zat(step), y, x, c) if kind[1] == "z" else dev(z, yat(step), x, c)
            return pltpu.make_async_remote_copy(
                src_ref=blk, dst_ref=blk, send_sem=ysend, recv_sem=yrecv.at[SEM_OF[key]],
                device_id=to, device_id_type=MESH)
        i = sems[2]
        return pltpu.make_async_remote_copy(
            src_ref=blk, dst_ref=blk, send_sem=sems[0].at[i], recv_sem=sems[1].at[i],
            device_id=to, device_id_type=pl.DeviceIdType.MESH)

    def arrive(key):
        kind = key[0]
        if kind == "X":
            blk = xblk(xat(-sgn(key[1]) * key[2]), c)
            sem = xrecv.at[XSEM_OF[key]]
        elif kind == "XS":
            blk = xblk(xat((0, 1, -1, 2)[key[1]]), 1 - c)
            sem = xrecv.at[XSEM_OF[key]]
        else:
            blk = block(key, key[3])
            sem = yrecv.at[SEM_OF[key]]
        pltpu.make_async_copy(blk, blk, sem).wait()

    def add_squares(blk_ref, first):
        v = blk_ref[...].astype(F32)
        sq[...] = v * v if first else sq[...] + v * v

    def dot_strip(half, strip):
        cols = pl.ds(pl.multiple_of(strip * STRIP, STRIP), STRIP)
        rows = [pl.ds(pl.multiple_of(zat(k) * 128, 128), 128) for k in DEPTHS[half]]
        lhs = jnp.concatenate([xb[:, r] for r in rows], axis=1)
        rhs = jnp.concatenate([yt[r, cols] for r in rows], axis=0)
        v = CROSS_SCALE * jnp.dot(lhs, rhs, preferred_element_type=F32)
        if half == 0:
            a = m_b[...]
            s_ref[:, cols] = v + jnp.concatenate([a, a], axis=1)
            return
        v = s_ref[:, cols] + v
        s_ref[:, cols] = v
        peak = jnp.max(jnp.max(v.reshape(ROWS // 8, 8, STRIP), axis=0), axis=0, keepdims=True)
        total = jnp.zeros((8, STRIP), F32)
        for r in range(0, ROWS, 256):
            e = exp2(s_ref[r:r + 256, cols] - peak)
            total = total + jnp.sum(e.reshape(32, 8, STRIP), axis=0)
        lse = peak + jnp.log2(jnp.sum(total, axis=0, keepdims=True))
        for h in range(STRIP // 128):
            colw[pl.ds(strip * (STRIP // 128) + h, 1), :] = lse[:, h * 128:(h + 1) * 128]

    def dense_into(ref, row, n):
        for k in range(n):
            ref[k:k + 1, :] = row[:, k * 128:(k + 1) * 128]

    def to_all_noise(buf, i):
        for dz, dy in FAR_FIRST:
            pltpu.make_async_remote_copy(
                src_ref=buf.at[noise], dst_ref=buf.at[noise], send_sem=csend.at[i], recv_sem=crecv.at[i],
                device_id=dev(zat(dz), yat(dy), x, c), device_id_type=MESH).start()

    def from_all_noise(buf, i):
        part = buf.at[pl.ds(0, NZ * NY - 1)]
        pltpu.make_async_copy(part, part, crecv.at[i]).wait()

    def send_on(kind, g, held, slot=(), only="pq"):
        for o in only:
            for (direction, dist), at in HELD_AT[kind].items():
                if direction == o and at == held:
                    desc((kind, g, o, dist) + slot).start()

    def handle(key):
        kind = key[0]
        if kind == "norm":
            m_b[...] = jnp.broadcast_to(-NORM_SCALE * jnp.sum(sq[...], axis=1, keepdims=True), (ROWS, 128))
            return
        if kind == "go":
            g = key[1]
            near, far = ("Az", "Ay") if GROUPS[g][0] == "A" else ("By", "Bz")
            send_on(near, g, 0)
            send_on(far, g, 0, (0,))
            return
        arrive(key)
        if kind in ("Az", "By"):
            g, pq, d = key[1:]
            send_on(kind, g, d, only=pq)
            if kind == "Az":
                send_on("Ay", g, 0, (-sgn(pq) * d,))
            else:
                send_on("Bz", g, 0, (2 if d == 2 else -sgn(pq),))
        elif kind in ("Ay", "Bz"):
            g, pq, d, slot = key[1:]
            send_on(kind, g, d, (slot,), only=pq)
        elif kind == "X":
            if key == ("X", "p", 1):
                desc(("X", "p", 2)).start()
            desc(("XS", {("p", 1): 1, ("q", 1): 2, ("p", 2): 3}[key[1:]])).start()
            add_squares(xblk(xat(-sgn(key[1]) * key[2]), c), False)
        elif kind == "XS":
            add_squares(xblk(xat((0, 1, -1, 2)[key[1]]), 1 - c), False)

    for g in range(len(GROUPS)):
        handle(("go", g))
    load_x.wait()
    desc(("X", "p", 1)).start()
    desc(("X", "q", 1)).start()
    desc(("XS", 0)).start()
    add_squares(xblk(x, c), True)

    ahead, steps_now = [], []
    for key in GATHER:
        if key[0] == "go":
            continue
        if key[0] == "dot":
            ahead.append((key[1:], steps_now))
            steps_now = []
        else:
            steps_now.append(key)
    strips = COLS // STRIP
    assert [k for k, _ in ahead] == [(h, i) for h in range(2) for i in range(strips)] and not steps_now

    for half_no in range(2):
        def strip_body(i, carry, half_no=half_no):
            for j in range(strips):
                todo = ahead[half_no * strips + j][1]
                if todo and (half_no, j) != (0, 0):
                    @pl.when(i == j)
                    def _():
                        for key in todo:
                            handle(key)
            if half_no:
                @pl.when(i == strips // 2)
                def _():
                    cx1[noise] = colw[0:8, :]
                    to_all_noise(cx1, 0)
            dot_strip(half_no, i)
            return carry

        if half_no == 0:
            for key in ahead[0][1]:
                handle(key)
        lax.fori_loop(0, strips, strip_body, 0)
    cx4[noise] = colw[8:16, :]
    to_all_noise(cx4, 3)
    pending.append((cx1.at[pl.ds(0, NZ * NY - 1)], csend.at[0]))
    pending.append((cx4.at[pl.ds(0, NZ * NY - 1)], csend.at[3]))
    pending.append((yt.at[pl.ds(0, (NZ * NY - 1) * 32), pl.ds(0, sum(g[2] for g in GROUPS))], ysend))
    for i in range(len(XKEYS)):
        pending.append((xblk(x, c), xsend.at[i]))

    def to_all_dp(buf, i):
        for dx, dc in ((2, 0), (2, 1), (1, 0), (1, 1), (-1, 0), (-1, 1), (0, 1)):
            pltpu.make_async_remote_copy(
                src_ref=buf.at[dp], dst_ref=buf.at[dp], send_sem=rsend.at[i], recv_sem=rrecv.at[i],
                device_id=dev(z, y, xat(dx), 1 - c if dc else c), device_id_type=MESH).start()
        pending.append((buf.at[pl.ds(0, NX * NC - 1)], rsend.at[i]))

    def from_all_dp(buf, i):
        part = buf.at[pl.ds(0, NX * NC - 1)]
        pltpu.make_async_copy(part, part, rrecv.at[i]).wait()

    def row_of(ref, n):
        return jnp.concatenate([ref[k:k + 1, :] for k in range(n)], axis=1)

    def stacked(row):
        n = row.shape[1]
        hi = row.astype(BF).astype(F32)
        lo = row - hi
        i = lax.broadcasted_iota(jnp.int32, (16, n), 0)
        return jnp.where(i == 0, jnp.broadcast_to(hi, (16, n)), jnp.where(i == 1, jnp.broadcast_to(lo, (16, n)), 0.0)).astype(BF)

    def lse_of(buf):
        v = buf[...]
        peak = jnp.max(v, axis=0)
        return peak + jnp.log2(jnp.sum(exp2(v - peak[None]), axis=0))

    def spread(ref, out):
        for b in range(ROWS // 128):
            out[b * 128:(b + 1) * 128, :] = jnp.broadcast_to(ref[b:b + 1, :], (128, 128)).T

    from_all_noise(cx1, 0)
    lse_a = lse_of(cx1)
    from_all_noise(cx4, 3)
    lse_b = lse_of(cx4)
    colw[0:8, :] = lse_a
    colw[8:16, :] = lse_b
    col1 = -math.log2(NM) - colw[...]
    colw[...] = col1

    col_row = row_of(colw, 16)

    def lane_tiles(v):
        return [v[:, k * 128:(k + 1) * 128] for k in range(COLS // 128)]

    def tree(op, parts):
        while len(parts) > 1:
            parts = [op(*parts[i:i + 2]) for i in range(0, len(parts), 2)]
        return parts[0]

    def row_peaks(i, carry):
        rows = pl.ds(pl.multiple_of(i * 16, 16), 16)
        l_b[rows, :] = tree(jnp.maximum, lane_tiles(s_ref[rows, :] + col_row))
        return carry

    lax.fori_loop(0, ROWS // 16, row_peaks, 0, unroll=4)
    for b in range(ROWS // 128):
        blk = pl.ds(b * 128, 128)
        t = l_b[blk, :]
        m_b[blk, :] = jnp.broadcast_to(jnp.max(t, axis=1, keepdims=True), (128, 128))
        roww[0, b:b + 1, :] = jnp.max(t.T, axis=0, keepdims=True)

    def row_exps(i, carry):
        rows = pl.ds(pl.multiple_of(i * 16, 16), 16)
        peak = m_b[rows, :]
        parts = [exp2(v - peak) for v in lane_tiles(s_ref[rows, :] + col_row)]
        for k, e in enumerate(parts):
            e_ref[rows, k * 128:(k + 1) * 128] = e.astype(BF)
        l_b[rows, :] = tree(jnp.add, parts)
        return carry

    lax.fori_loop(0, ROWS // 16, row_exps, 0, unroll=4)
    for b in range(ROWS // 128):
        t = l_b[b * 128:(b + 1) * 128, :].T
        roww[1, b:b + 1, :] = jnp.sum(t, axis=0, keepdims=True)
    roww[1] = roww[0] + jnp.log2(roww[1])
    rx1[dp] = roww[1]
    to_all_dp(rx1, 0)
    from_all_dp(rx1, 0)
    lse1 = lse_of(rx1)
    g = exp2(roww[0] - lse1)
    row1 = -math.log2(NN) - lse1
    roww[0] = g

    def col_sums(buf, stage, i, u):
        roww[1] = u
        q = jnp.dot(stacked(row_of(roww.at[1], 8)), e_ref[...], preferred_element_type=F32)
        dense_into(colw, q[0:1, :] + q[1:2, :], 16)
        stage[...] = colw[...]
        buf[noise] = stage[...].astype(BF)
        to_all_noise(buf, i)
        pending.append((buf.at[pl.ds(0, NZ * NY - 1)], csend.at[i]))

    def row_sums(v, buf, i):
        colw[...] = v
        q = lax.dot_general(stacked(row_of(colw, 16)), e_ref[...], (((1,), (1,)), ((), ())), preferred_element_type=F32)
        dense_into(roww.at[1], q[0:1, :] + q[1:2, :], 8)
        buf[dp] = roww[1] * roww[0]
        to_all_dp(buf, i)

    col_sums(cx2, cs2, 1, g)
    spread(roww.at[0], g_b)
    norms = jnp.zeros((1, COLS), F32)
    def col_norm(i, carry):
        v = yt[pl.ds(pl.multiple_of(i * 32, 32), 32), :].astype(F32)
        return carry + jnp.sum((v * v).reshape(4, 8, COLS), axis=0)
    norms = jnp.sum(lax.fori_loop(0, D // 32, col_norm, jnp.zeros((8, COLS), F32)), axis=0, keepdims=True)
    dense_into(cs3, norms, 16)
    from_all_noise(cx2, 1)
    row_sums(1.0 / jnp.sum(cx2[...].astype(F32), axis=0), rx2, 1)
    from_all_dp(rx2, 1)
    t2 = jnp.sum(rx2[...], axis=0)

    col_sums(cx3, cs2, 2, roww[0] / t2)
    from_all_noise(cx3, 2)
    q3 = jnp.sum(cx3[...].astype(F32), axis=0)
    v3 = 1.0 / q3
    col_out[...] = (EPSILON / LOG2E) * (col1 + 2.0 - jnp.log2(q3) + NORM_SCALE * cs3[...])
    colw[...] = v3
    v_row = row_of(colw, 16)

    half = pl.ds(0, ROWS // 2), pl.ds(ROWS // 2, ROWS // 2)
    right, left = dev(z, y, lax.rem(x + 1, NX), c), dev(z, y, lax.rem(x + NX - 1, NX), c)

    def rcopy(src, dst, i, to):
        return pltpu.make_async_remote_copy(
            src_ref=src, dst_ref=dst, send_sem=fsend.at[i], recv_sem=frecv.at[i],
            device_id=to, device_id_type=pl.DeviceIdType.MESH)

    def sib_copy(k, h):
        return pltpu.make_async_remote_copy(
            src_ref=sib_s.at[k, half[h]], dst_ref=sib_r.at[k, half[h]], send_sem=psend.at[2 * k + h], recv_sem=precv.at[2 * k + h],
            device_id=dev(z, y, x, 1 - c), device_id_type=MESH)

    def weigh(k, h):
        first = lax.rem(x + 2 + 3 * k + 3 * (k // 2) + 2 * (k // 3), NX) * 256

        @pl.when(h == 0)
        def _():
            def body(i, carry):
                rows = pl.ds(pl.multiple_of(first + i * 32, 32), 32)
                vy[rows, :] = (yt[rows, :].astype(F32) * v_row).astype(BF)
                return carry

            lax.fori_loop(0, 8, body, 0)

        w = vy[pl.ds(pl.multiple_of(first, 256), 256), :]
        rows = pl.ds(pl.multiple_of(h * (ROWS // 2), ROWS // 2), ROWS // 2)
        p = lax.dot_general(e_ref[rows, :], w, (((1,), (1,)), ((), ())), preferred_element_type=F32)
        gg = g_b[rows, :]
        lo, hi = p[:, :128] * gg, p[:, 128:] * gg
        acc[k, rows, :] = jnp.where(c == 0, lo, hi)
        sib_s[k, rows, :] = jnp.where(c == 0, hi, lo).astype(BF)

    def presum(k, h):
        sib_copy(k, h).wait_recv()
        return acc[k, half[h], :] + sib_r[k, half[h], :].astype(F32)

    far = [rcopy(far_s.at[half[0]], far_r.at[0], 0, right), rcopy(far_s.at[half[1]], far_r.at[1], 1, left)]
    near0 = rcopy(near_s.at[0], near_r.at[0], 2, right)
    near1 = rcopy(near_s.at[1], near_r.at[1], 3, left)
    mrg0 = rcopy(mrg_s.at[0], mrg_r.at[0], 4, right)
    mrg1 = rcopy(mrg_s.at[1], mrg_r.at[1], 5, left)
    def far_go(h):
        far_s[half[h], :] = presum(0, h).astype(BF)
        far[h].start()

    def near0_go():
        near_s[0] = presum(1, 1).astype(BF)
        near0.start()

    def near1_go():
        near_s[1] = presum(2, 0).astype(BF)
        near1.start()

    after = {2: lambda: far_go(0), 3: lambda: far_go(1), 5: near0_go, 6: near1_go}

    def weigh_body(i, carry):
        weigh(i // 2, i % 2)
        for j in range(8):
            @pl.when(i == j)
            def _():
                sib_copy(j // 2, j % 2).start()
                if j in after:
                    after[j]()
        return carry

    lax.fori_loop(0, 8, weigh_body, 0)
    row_sums(v3, rx3, 2)
    far[0].wait_recv()
    mrg_s[0] = (presum(1, 0) + far_r[0].astype(F32)).astype(BF)
    mrg0.start()
    far[1].wait_recv()
    mrg_s[1] = (presum(2, 1) + far_r[1].astype(F32)).astype(BF)
    mrg1.start()
    acc[3, half[0], :] = presum(3, 0)
    acc[3, half[1], :] = presum(3, 1)
    from_all_dp(rx3, 2)
    t3 = jnp.sum(rx3[...], axis=0)
    row_out[...] = (EPSILON / LOG2E) * (row1 - 2.0 - jnp.log2(t3))
    roww[1] = 1.0 / t3
    spread(roww.at[1], t_b)
    near0.wait_recv()
    near1.wait_recv()
    mrg0.wait_recv()
    tgt_out[half[0], :] = ((acc[3, half[0], :] + near_r[1].astype(F32) + mrg_r[0].astype(F32)) * t_b[half[0], :]).astype(BF)
    mrg1.wait_recv()
    tgt_out[half[1], :] = ((acc[3, half[1], :] + near_r[0].astype(F32) + mrg_r[1].astype(F32)) * t_b[half[1], :]).astype(BF)

    for d in far + [near0, near1, mrg0, mrg1]:
        d.wait_send()
    for k in range(4):
        for h in range(2):
            sib_copy(k, h).wait_send()
    finish()


def place(row_in, col_in, tgt_in, row_out, col_out, tgt_out):
    row_out[...] = row_in[...]
    col_out[...] = col_in[...]
    tgt_out[...] = tgt_in[...]


def local(noise_batch, latents):
    v = pltpu.VMEM
    dma = pltpu.SemaphoreType.DMA
    row, col, tgt = pl.pallas_call(
        kernel,
        out_shape=(
            jax.ShapeDtypeStruct((8, 128), F32),
            jax.ShapeDtypeStruct((16, 128), F32),
            jax.ShapeDtypeStruct((ROWS, 128), BF),
        ),
        in_specs=[pl.BlockSpec(memory_space=pl.ANY)] * 2,
        out_specs=[pl.BlockSpec(memory_space=pltpu.VMEM)] * 3,
        scratch_shapes=[
            v((D, COLS), BF),
            v((ROWS, D), BF),
            v((ROWS, COLS), F32),
            v((ROWS, COLS), BF),
            v((D, COLS), BF),
            v((ROWS, 128), F32),
            v((ROWS, 128), F32),
            v((ROWS, 128), F32),
            v((ROWS, 128), F32),
            v((ROWS, 128), F32),
            v((16, 128), F32),
            v((2, 8, 128), F32),
            v((32, 8, 128), F32),
            v((32, 16, 128), BF),
            v((32, 16, 128), BF),
            v((32, 8, 128), F32),
            v((16, 128), F32),
            v((16, 128), F32),
            v((8, 8, 128), F32),
            v((8, 8, 128), F32),
            v((8, 8, 128), F32),
            v((4, ROWS, 128), BF),
            v((4, ROWS, 128), BF),
            v((4, ROWS, 128), F32),
            v((ROWS, 128), BF),
            v((2, ROWS // 2, 128), BF),
            v((2, ROWS // 2, 128), BF),
            v((2, ROWS // 2, 128), BF),
            v((2, ROWS // 2, 128), BF),
            v((2, ROWS // 2, 128), BF),
            dma((2,)),
            dma,
            dma((len(KEYS),)),
            dma((len(XKEYS),)),
            dma((len(XKEYS),)),
            dma((4,)),
            dma((4,)),
            dma((3,)),
            dma((3,)),
            dma((8,)),
            dma((8,)),
            dma((6,)),
            dma((6,)),
        ],
        compiler_params=pltpu.CompilerParams(
            collective_id=0, has_side_effects=True, vmem_limit_bytes=56 * 2**20),
        cost_estimate=pl.CostEstimate(flops=4 * ROWS * COLS * D, bytes_accessed=2**20, transcendentals=2 * ROWS * COLS),
    )(noise_batch, latents.T)
    row, col, tgt = pl.pallas_call(
        place,
        out_shape=(
            jax.ShapeDtypeStruct((8, 128), F32),
            jax.ShapeDtypeStruct((16, 128), F32),
            jax.ShapeDtypeStruct((ROWS, 128), BF),
        ),
        in_specs=[pl.BlockSpec(memory_space=pltpu.VMEM)] * 3,
        out_specs=[pl.BlockSpec(memory_space=pltpu.VMEM)] * 3,
        compiler_params=pltpu.CompilerParams(vmem_limit_bytes=60 * 2**20),
    )(row, col, tgt)
    return row.reshape(ROWS), col.reshape(COLS), tgt


def solution(mesh):
    in_specs = (P("noise", "dp"), P("dp", "noise"))
    out_specs = (P("noise"), P("dp"), P("noise", "dp"))
    return jax.shard_map(local, mesh=mesh, in_specs=in_specs, out_specs=out_specs, check_vma=False)
```

```python
import math

import jax
import jax.numpy as jnp
from jax import lax
from jax.experimental import pallas as pl
from jax.experimental.pallas import tpu as pltpu
from jax.sharding import PartitionSpec as P

EPSILON = 0.01
NZ, NY, NX, NC = 8, 4, 4, 2
ROWS, COLS, D = 1024, 2048, 1024
NN, NM = 32768, 16384
LOG2E = math.log2(math.e)
NORM_SCALE = LOG2E / (EPSILON * D)
CROSS_SCALE = 2.0 * NORM_SCALE
STRIP = 256

BF = jnp.bfloat16
F32 = jnp.float32

HELD_AT = {
    'Az': {('p', 1): 0, ('p', 2): 1, ('p', 3): 2, ('p', 4): 3, ('q', 1): 0, ('q', 2): 1, ('q', 3): 2},
    'By': {('p', 1): 0, ('q', 1): 0, ('p', 2): 1},
    'Ay': {('p', 1): 0, ('q', 1): 0, ('p', 2): 1},
    'Bz': {('p', 1): 0, ('p', 2): 1, ('p', 3): 2, ('p', 4): 3, ('q', 1): 0, ('q', 2): 1, ('q', 3): 2},
}
GROUPS = (('A', 0, 768), ('B', 768, 256), ('A', 1024, 512), ('B', 1536, 512))
GATHER = (
    ('go', 0), ('go', 1), ('go', 2), ('go', 3), ('XS', 0), ('Az', 0, 'p', 1), ('Az', 0, 'q', 1), ('Ay', 0, 'p', 1, 0),
    ('Ay', 0, 'q', 1, 0), ('Bz', 1, 'p', 1, 0), ('Bz', 1, 'q', 1, 0), ('By', 1, 'p', 1), ('By', 1, 'q', 1),
    ('Az', 2, 'p', 1), ('Az', 2, 'q', 1), ('Ay', 2, 'p', 1, 0), ('Ay', 2, 'q', 1, 0), ('Bz', 3, 'p', 1, 0),
    ('Bz', 3, 'q', 1, 0), ('By', 3, 'p', 1), ('By', 3, 'q', 1), ('Az', 0, 'p', 2), ('Ay', 0, 'p', 1, -1),
    ('Ay', 0, 'q', 1, -1), ('Az', 0, 'q', 2), ('Ay', 0, 'p', 1, 1), ('Ay', 0, 'q', 1, 1), ('Bz', 1, 'p', 2, 0),
    ('Bz', 1, 'q', 2, 0), ('Bz', 1, 'p', 1, -1), ('X', 'p', 1), ('Bz', 1, 'q', 1, -1), ('X', 'q', 1),
    ('Bz', 1, 'p', 1, 1), ('Ay', 0, 'p', 2, 0), ('Bz', 1, 'q', 1, 1), ('Az', 2, 'p', 2), ('Az', 2, 'q', 2),
    ('By', 1, 'p', 2), ('XS', 1), ('Bz', 3, 'p', 2, 0), ('Ay', 2, 'p', 1, -1), ('XS', 2), ('Ay', 2, 'q', 1, -1),
    ('Bz', 3, 'q', 2, 0), ('Bz', 3, 'p', 1, -1), ('Ay', 2, 'p', 1, 1), ('Ay', 2, 'q', 1, 1), ('Bz', 3, 'q', 1, -1),
    ('Bz', 3, 'p', 1, 1), ('Ay', 2, 'p', 2, 0), ('Bz', 3, 'q', 1, 1), ('By', 3, 'p', 2), ('Az', 0, 'p', 3),
    ('Ay', 0, 'p', 1, -2), ('Ay', 0, 'q', 1, -2), ('Az', 0, 'q', 3), ('Ay', 0, 'p', 2, -1), ('Ay', 0, 'q', 1, 2),
    ('Bz', 1, 'p', 3, 0), ('Bz', 1, 'q', 3, 0), ('Bz', 1, 'p', 2, -1), ('Bz', 1, 'q', 2, -1), ('Bz', 1, 'p', 2, 1),
    ('Ay', 0, 'p', 1, 2), ('Bz', 1, 'q', 2, 1), ('Az', 2, 'p', 3), ('Az', 2, 'q', 3), ('Ay', 0, 'p', 2, 1),
    ('Bz', 1, 'q', 1, 2), ('X', 'p', 2), ('Bz', 1, 'p', 1, 2), ('Bz', 3, 'p', 3, 0), ('Ay', 2, 'p', 1, -2),
    ('Ay', 2, 'q', 1, -2), ('Bz', 3, 'q', 3, 0), ('Bz', 3, 'p', 2, -1), ('Ay', 2, 'p', 1, 2), ('Ay', 2, 'q', 1, 2),
    ('Bz', 3, 'q', 2, -1), ('Bz', 3, 'p', 2, 1), ('Bz', 3, 'q', 2, 1), ('XS', 3), ('norm',), ('Ay', 2, 'p', 2, -1),
    ('Ay', 2, 'p', 2, 1), ('Bz', 3, 'q', 1, 2), ('Bz', 3, 'p', 1, 2), ('Ay', 0, 'p', 1, -3), ('Ay', 0, 'q', 1, -3),
    ('Ay', 0, 'p', 2, -2), ('Ay', 0, 'q', 1, 3), ('Az', 0, 'p', 4), ('Bz', 1, 'p', 4, 0), ('Bz', 1, 'q', 3, -1),
    ('Bz', 1, 'p', 3, -1), ('Ay', 0, 'p', 1, 3), ('Bz', 1, 'q', 3, 1), ('Bz', 1, 'p', 3, 1), ('Bz', 1, 'q', 2, 2),
    ('Az', 2, 'p', 4), ('Bz', 1, 'p', 2, 2), ('dot', 0, 0), ('Bz', 3, 'p', 4, 0), ('dot', 0, 1), ('Ay', 0, 'p', 2, 2),
    ('Bz', 3, 'q', 3, -1), ('Bz', 3, 'p', 3, -1), ('Ay', 2, 'p', 1, -3), ('Ay', 2, 'q', 1, -3), ('dot', 0, 2),
    ('Bz', 3, 'q', 3, 1), ('Bz', 3, 'p', 3, 1), ('Ay', 2, 'p', 1, 3), ('Ay', 2, 'q', 1, 3), ('Bz', 3, 'q', 2, 2),
    ('dot', 0, 3), ('Bz', 3, 'p', 2, 2), ('Ay', 2, 'p', 2, -2), ('Ay', 2, 'p', 2, 2), ('dot', 0, 4),
    ('Bz', 1, 'p', 4, -1), ('Bz', 1, 'p', 4, 1), ('Bz', 1, 'p', 3, 2), ('dot', 0, 5), ('Ay', 0, 'p', 2, -3),
    ('Ay', 0, 'q', 1, -4), ('Bz', 1, 'q', 3, 2), ('Ay', 0, 'p', 1, -4), ('dot', 0, 6), ('Bz', 3, 'p', 4, -1),
    ('Bz', 3, 'p', 4, 1), ('Ay', 0, 'p', 2, 3), ('dot', 0, 7), ('Bz', 3, 'q', 3, 2), ('Ay', 2, 'p', 1, -4),
    ('Bz', 3, 'p', 3, 2), ('Ay', 2, 'q', 1, -4), ('Ay', 2, 'p', 2, -3), ('Bz', 1, 'p', 4, 2), ('Ay', 2, 'p', 2, 3),
    ('Ay', 0, 'p', 2, -4), ('dot', 1, 0), ('Ay', 2, 'p', 2, -4), ('dot', 1, 1), ('Bz', 3, 'p', 4, 2), ('dot', 1, 2),
    ('dot', 1, 3), ('dot', 1, 4), ('dot', 1, 5), ('dot', 1, 6), ('dot', 1, 7),
)
DEPTHS = ((0, -1, 1, -2), (2, -3, 3, -4))
KEYS = [e for e in GATHER if e[0] in ("Az", "Ay", "By", "Bz")]
assert len(set(KEYS)) == len(KEYS) == 31 * len(GROUPS)
SEM_OF = {k: i for i, k in enumerate(KEYS)}
XKEYS = [("X", "p", 1), ("X", "q", 1), ("X", "p", 2), ("XS", 0), ("XS", 1), ("XS", 2), ("XS", 3)]
XSEM_OF = {k: i for i, k in enumerate(XKEYS)}

FAR_FIRST = sorted(
    ((dz, dy) for dz in range(-3, 5) for dy in range(-1, 3) if dz or dy),
    key=lambda p: (-abs(p[0]) - abs(p[1]), p))


def exp2(v):
    return jnp.exp2(v)


def kernel(noise_ref, lat_ref, row_out, col_out, tgt_out,
           yt, xb, s_ref, e_ref, vy, sq, m_b, l_b, g_b, t_b, colw, roww,
           cx1, cx2, cx3, cx4, cs2, cs3, rx1, rx2, rx3,
           sib_s, sib_r, acc, far_s, far_r, near_s, near_r, mrg_s, mrg_r,
           in_sem, ysend, yrecv, xsend, xrecv, csend, crecv, rsend, rrecv, psend, precv, fsend, frecv):
    noise = lax.axis_index("noise")
    dp = lax.axis_index("dp")
    z, y = noise // NY, noise % NY
    x, c = dp // NC, dp % NC
    s = 1 - 2 * c

    def dev(zz, yy, xx, cc):
        return {"noise": zz * NY + yy, "dp": xx * NC + cc}

    def zat(k):
        return lax.rem(z + s * k + 2 * NZ, NZ)

    def yat(k):
        return lax.rem(y + s * k + 2 * NY, NY)

    def xat(k):
        return lax.rem(x + s * k + 2 * NX, NX)

    def yrow(zz, yy):
        return pl.multiple_of(zz * 128 + yy * 32, 32)

    own_x = pl.multiple_of(dp * 128, 128)
    load_lat = pltpu.make_async_copy(lat_ref, yt.at[pl.ds(yrow(z, y), 32), :], in_sem.at[0])
    load_x = pltpu.make_async_copy(noise_ref, xb.at[:, pl.ds(own_x, 128)], in_sem.at[1])
    load_lat.start()
    load_x.start()

    MESH = pl.DeviceIdType.MESH
    barrier = pltpu.get_barrier_semaphore()
    around = [dev(zat(1), y, x, c), dev(zat(-1), y, x, c), dev(z, yat(1), x, c), dev(z, yat(-1), x, c),
              dev(z, y, xat(1), c), dev(z, y, xat(-1), c), dev(z, y, x, 1 - c)]
    for to in around:
        pl.semaphore_signal(barrier, 1, device_id=to, device_id_type=MESH)

    load_lat.wait()
    load_x.wait()
    pl.semaphore_wait(barrier, len(around))

    pending = []

    def finish():
        for part, sem in pending:
            pltpu.make_async_copy(part, part, sem).wait()

    def xblk(xx, cc):
        return xb.at[:, pl.ds(pl.multiple_of((xx * NC + cc) * 128, 128), 128)]

    def sgn(pq):
        return 1 if pq == "p" else -1

    def block(key, dist):
        kind, g, o = key[0], key[1], sgn(key[2])
        if kind == "Az":
            at = zat(-o * dist), y
        elif kind == "Ay":
            at = zat(key[4]), yat(-o * dist)
        elif kind == "By":
            at = z, yat(-o * dist)
        else:
            at = zat(-o * dist), yat(key[4])
        return yt.at[pl.ds(yrow(*at), 32), pl.ds(GROUPS[g][1], GROUPS[g][2])]

    def desc(key):
        kind = key[0]
        if kind == "X":
            o = sgn(key[1])
            blk = xblk(xat(-o * (key[2] - 1)), c)
            to = dev(z, y, xat(o), c)
            sems = xsend, xrecv, XSEM_OF[key]
        elif kind == "XS":
            blk = xblk(xat((0, -1, 1, -2)[key[1]]), c)
            to = dev(z, y, x, 1 - c)
            sems = xsend, xrecv, XSEM_OF[key]
        else:
            o = sgn(key[2])
            held = HELD_AT[kind][key[2:4]]
            blk = block(key, held)
            step = o * (key[3] - held)
            to = dev(zat(step), y, x, c) if kind[1] == "z" else dev(z, yat(step), x, c)
            return pltpu.make_async_remote_copy(
                src_ref=blk, dst_ref=blk, send_sem=ysend, recv_sem=yrecv.at[SEM_OF[key]],
                device_id=to, device_id_type=MESH)
        i = sems[2]
        return pltpu.make_async_remote_copy(
            src_ref=blk, dst_ref=blk, send_sem=sems[0].at[i], recv_sem=sems[1].at[i],
            device_id=to, device_id_type=pl.DeviceIdType.MESH)

    def arrive(key):
        kind = key[0]
        if kind == "X":
            blk = xblk(xat(-sgn(key[1]) * key[2]), c)
            sem = xrecv.at[XSEM_OF[key]]
        elif kind == "XS":
            blk = xblk(xat((0, 1, -1, 2)[key[1]]), 1 - c)
            sem = xrecv.at[XSEM_OF[key]]
        else:
            blk = block(key, key[3])
            sem = yrecv.at[SEM_OF[key]]
        pltpu.make_async_copy(blk, blk, sem).wait()

    def add_squares(blk_ref, first):
        v = blk_ref[...].astype(F32)
        sq[...] = v * v if first else sq[...] + v * v

    def dot_strip(half, strip):
        cols = pl.ds(pl.multiple_of(strip * STRIP, STRIP), STRIP)
        rows = [pl.ds(pl.multiple_of(zat(k) * 128, 128), 128) for k in DEPTHS[half]]
        lhs = jnp.concatenate([xb[:, r] for r in rows], axis=1)
        rhs = jnp.concatenate([yt[r, cols] for r in rows], axis=0)
        v = CROSS_SCALE * jnp.dot(lhs, rhs, preferred_element_type=F32)
        if half == 0:
            a = m_b[...]
            s_ref[:, cols] = v + jnp.concatenate([a, a], axis=1)
            return
        v = s_ref[:, cols] + v
        s_ref[:, cols] = v
        peak = jnp.max(jnp.max(v.reshape(ROWS // 8, 8, STRIP), axis=0), axis=0, keepdims=True)
        total = jnp.zeros((8, STRIP), F32)
        for r in range(0, ROWS, 256):
            e = exp2(s_ref[r:r + 256, cols] - peak)
            total = total + jnp.sum(e.reshape(32, 8, STRIP), axis=0)
        lse = peak + jnp.log2(jnp.sum(total, axis=0, keepdims=True))
        for h in range(STRIP // 128):
            colw[pl.ds(strip * (STRIP // 128) + h, 1), :] = lse[:, h * 128:(h + 1) * 128]

    def dense_into(ref, row, n):
        for k in range(n):
            ref[k:k + 1, :] = row[:, k * 128:(k + 1) * 128]

    def to_all_noise(buf, i):
        for dz, dy in FAR_FIRST:
            pltpu.make_async_remote_copy(
                src_ref=buf.at[noise], dst_ref=buf.at[noise], send_sem=csend.at[i], recv_sem=crecv.at[i],
                device_id=dev(zat(dz), yat(dy), x, c), device_id_type=MESH).start()

    def from_all_noise(buf, i):
        part = buf.at[pl.ds(0, NZ * NY - 1)]
        pltpu.make_async_copy(part, part, crecv.at[i]).wait()

    desc(("X", "p", 1)).start()
    desc(("X", "q", 1)).start()
    desc(("XS", 0)).start()
    add_squares(xblk(x, c), True)

    def send_on(kind, g, held, slot=(), only="pq"):
        for o in only:
            for (direction, dist), at in HELD_AT[kind].items():
                if direction == o and at == held:
                    desc((kind, g, o, dist) + slot).start()

    def handle(key):
        kind = key[0]
        if kind == "norm":
            m_b[...] = jnp.broadcast_to(-NORM_SCALE * jnp.sum(sq[...], axis=1, keepdims=True), (ROWS, 128))
            return
        if kind == "go":
            g = key[1]
            near, far = ("Az", "Ay") if GROUPS[g][0] == "A" else ("By", "Bz")
            send_on(near, g, 0)
            send_on(far, g, 0, (0,))
            return
        arrive(key)
        if kind in ("Az", "By"):
            g, pq, d = key[1:]
            send_on(kind, g, d, only=pq)
            if kind == "Az":
                send_on("Ay", g, 0, (-sgn(pq) * d,))
            else:
                send_on("Bz", g, 0, (2 if d == 2 else -sgn(pq),))
        elif kind in ("Ay", "Bz"):
            g, pq, d, slot = key[1:]
            send_on(kind, g, d, (slot,), only=pq)
        elif kind == "X":
            if key == ("X", "p", 1):
                desc(("X", "p", 2)).start()
            desc(("XS", {("p", 1): 1, ("q", 1): 2, ("p", 2): 3}[key[1:]])).start()
            add_squares(xblk(xat(-sgn(key[1]) * key[2]), c), False)
        elif kind == "XS":
            add_squares(xblk(xat((0, 1, -1, 2)[key[1]]), 1 - c), False)

    ahead, steps_now = [], []
    for key in GATHER:
        if key[0] == "dot":
            ahead.append((key[1:], steps_now))
            steps_now = []
        else:
            steps_now.append(key)
    strips = COLS // STRIP
    assert [k for k, _ in ahead] == [(h, i) for h in range(2) for i in range(strips)] and not steps_now

    for half_no in range(2):
        def strip_body(i, carry, half_no=half_no):
            for j in range(strips):
                todo = ahead[half_no * strips + j][1]
                if todo and (half_no, j) != (0, 0):
                    @pl.when(i == j)
                    def _():
                        for key in todo:
                            handle(key)
            if half_no:
                @pl.when(i == strips // 2)
                def _():
                    cx1[noise] = colw[0:8, :]
                    to_all_noise(cx1, 0)
            dot_strip(half_no, i)
            return carry

        if half_no == 0:
            for key in ahead[0][1]:
                handle(key)
        lax.fori_loop(0, strips, strip_body, 0)
    cx4[noise] = colw[8:16, :]
    to_all_noise(cx4, 3)
    pending.append((cx1.at[pl.ds(0, NZ * NY - 1)], csend.at[0]))
    pending.append((cx4.at[pl.ds(0, NZ * NY - 1)], csend.at[3]))
    pending.append((yt.at[pl.ds(0, (NZ * NY - 1) * 32), pl.ds(0, sum(g[2] for g in GROUPS))], ysend))
    for i in range(len(XKEYS)):
        pending.append((xblk(x, c), xsend.at[i]))

    def to_all_dp(buf, i):
        for dx, dc in ((2, 0), (2, 1), (1, 0), (1, 1), (-1, 0), (-1, 1), (0, 1)):
            pltpu.make_async_remote_copy(
                src_ref=buf.at[dp], dst_ref=buf.at[dp], send_sem=rsend.at[i], recv_sem=rrecv.at[i],
                device_id=dev(z, y, xat(dx), 1 - c if dc else c), device_id_type=MESH).start()
        pending.append((buf.at[pl.ds(0, NX * NC - 1)], rsend.at[i]))

    def from_all_dp(buf, i):
        part = buf.at[pl.ds(0, NX * NC - 1)]
        pltpu.make_async_copy(part, part, rrecv.at[i]).wait()

    def row_of(ref, n):
        return jnp.concatenate([ref[k:k + 1, :] for k in range(n)], axis=1)

    def stacked(row):
        n = row.shape[1]
        hi = row.astype(BF).astype(F32)
        lo = row - hi
        i = lax.broadcasted_iota(jnp.int32, (16, n), 0)
        return jnp.where(i == 0, jnp.broadcast_to(hi, (16, n)), jnp.where(i == 1, jnp.broadcast_to(lo, (16, n)), 0.0)).astype(BF)

    def lse_of(buf):
        v = buf[...]
        peak = jnp.max(v, axis=0)
        return peak + jnp.log2(jnp.sum(exp2(v - peak[None]), axis=0))

    def spread(ref, out):
        for b in range(ROWS // 128):
            out[b * 128:(b + 1) * 128, :] = jnp.broadcast_to(ref[b:b + 1, :], (128, 128)).T

    from_all_noise(cx1, 0)
    lse_a = lse_of(cx1)
    from_all_noise(cx4, 3)
    lse_b = lse_of(cx4)
    colw[0:8, :] = lse_a
    colw[8:16, :] = lse_b
    col1 = -math.log2(NM) - colw[...]
    colw[...] = col1

    col_row = row_of(colw, 16)

    def lane_tiles(v):
        return [v[:, k * 128:(k + 1) * 128] for k in range(COLS // 128)]

    def tree(op, parts):
        while len(parts) > 1:
            parts = [op(*parts[i:i + 2]) for i in range(0, len(parts), 2)]
        return parts[0]

    def row_peaks(i, carry):
        rows = pl.ds(pl.multiple_of(i * 16, 16), 16)
        l_b[rows, :] = tree(jnp.maximum, lane_tiles(s_ref[rows, :] + col_row))
        return carry

    lax.fori_loop(0, ROWS // 16, row_peaks, 0, unroll=8)
    for b in range(ROWS // 128):
        blk = pl.ds(b * 128, 128)
        t = l_b[blk, :]
        m_b[blk, :] = jnp.broadcast_to(jnp.max(t, axis=1, keepdims=True), (128, 128))
        roww[0, b:b + 1, :] = jnp.max(t.T, axis=0, keepdims=True)

    def row_exps(i, carry):
        rows = pl.ds(pl.multiple_of(i * 16, 16), 16)
        peak = m_b[rows, :]
        parts = [exp2(v - peak) for v in lane_tiles(s_ref[rows, :] + col_row)]
        for k, e in enumerate(parts):
            e_ref[rows, k * 128:(k + 1) * 128] = e.astype(BF)
        l_b[rows, :] = tree(jnp.add, parts)
        return carry

    lax.fori_loop(0, ROWS // 16, row_exps, 0, unroll=8)
    for b in range(ROWS // 128):
        t = l_b[b * 128:(b + 1) * 128, :].T
        roww[1, b:b + 1, :] = jnp.sum(t, axis=0, keepdims=True)
    roww[1] = roww[0] + jnp.log2(roww[1])
    rx1[dp] = roww[1]
    to_all_dp(rx1, 0)
    from_all_dp(rx1, 0)
    lse1 = lse_of(rx1)
    g = exp2(roww[0] - lse1)
    row1 = -math.log2(NN) - lse1
    roww[0] = g

    def col_sums(buf, stage, i, u):
        roww[1] = u
        q = jnp.dot(stacked(row_of(roww.at[1], 8)), e_ref[...], preferred_element_type=F32)
        dense_into(colw, q[0:1, :] + q[1:2, :], 16)
        stage[...] = colw[...]
        buf[noise] = stage[...].astype(BF)
        to_all_noise(buf, i)
        pending.append((buf.at[pl.ds(0, NZ * NY - 1)], csend.at[i]))

    def row_sums(v, buf, i):
        colw[...] = v
        q = lax.dot_general(stacked(row_of(colw, 16)), e_ref[...], (((1,), (1,)), ((), ())), preferred_element_type=F32)
        dense_into(roww.at[1], q[0:1, :] + q[1:2, :], 8)
        buf[dp] = roww[1] * roww[0]
        to_all_dp(buf, i)

    col_sums(cx2, cs2, 1, g)
    spread(roww.at[0], g_b)
    norms = jnp.zeros((1, COLS), F32)
    def col_norm(i, carry):
        v = yt[pl.ds(pl.multiple_of(i * 32, 32), 32), :].astype(F32)
        return carry + jnp.sum((v * v).reshape(4, 8, COLS), axis=0)
    norms = jnp.sum(lax.fori_loop(0, D // 32, col_norm, jnp.zeros((8, COLS), F32)), axis=0, keepdims=True)
    dense_into(cs3, norms, 16)
    from_all_noise(cx2, 1)
    row_sums(1.0 / jnp.sum(cx2[...].astype(F32), axis=0), rx2, 1)
    from_all_dp(rx2, 1)
    t2 = jnp.sum(rx2[...], axis=0)

    col_sums(cx3, cs2, 2, roww[0] / t2)
    from_all_noise(cx3, 2)
    q3 = jnp.sum(cx3[...].astype(F32), axis=0)
    v3 = 1.0 / q3
    col_out[...] = (EPSILON / LOG2E) * (col1 + 2.0 - jnp.log2(q3) + NORM_SCALE * cs3[...])
    colw[...] = v3
    v_row = row_of(colw, 16)

    half = pl.ds(0, ROWS // 2), pl.ds(ROWS // 2, ROWS // 2)
    right, left = dev(z, y, lax.rem(x + 1, NX), c), dev(z, y, lax.rem(x + NX - 1, NX), c)

    def rcopy(src, dst, i, to):
        return pltpu.make_async_remote_copy(
            src_ref=src, dst_ref=dst, send_sem=fsend.at[i], recv_sem=frecv.at[i],
            device_id=to, device_id_type=pl.DeviceIdType.MESH)

    def sib_copy(k, h):
        return pltpu.make_async_remote_copy(
            src_ref=sib_s.at[k, half[h]], dst_ref=sib_r.at[k, half[h]], send_sem=psend.at[2 * k + h], recv_sem=precv.at[2 * k + h],
            device_id=dev(z, y, x, 1 - c), device_id_type=MESH)

    def weigh(k, h):
        first = lax.rem(x + 2 + 3 * k + 3 * (k // 2) + 2 * (k // 3), NX) * 256

        @pl.when(h == 0)
        def _():
            def body(i, carry):
                rows = pl.ds(pl.multiple_of(first + i * 32, 32), 32)
                vy[rows, :] = (yt[rows, :].astype(F32) * v_row).astype(BF)
                return carry

            lax.fori_loop(0, 8, body, 0)

        w = vy[pl.ds(pl.multiple_of(first, 256), 256), :]
        rows = pl.ds(pl.multiple_of(h * (ROWS // 2), ROWS // 2), ROWS // 2)
        p = lax.dot_general(e_ref[rows, :], w, (((1,), (1,)), ((), ())), preferred_element_type=F32)
        gg = g_b[rows, :]
        lo, hi = p[:, :128] * gg, p[:, 128:] * gg
        acc[k, rows, :] = jnp.where(c == 0, lo, hi)
        sib_s[k, rows, :] = jnp.where(c == 0, hi, lo).astype(BF)

    def presum(k, h):
        sib_copy(k, h).wait_recv()
        return acc[k, half[h], :] + sib_r[k, half[h], :].astype(F32)

    far = [rcopy(far_s.at[half[0]], far_r.at[0], 0, right), rcopy(far_s.at[half[1]], far_r.at[1], 1, left)]
    near0 = rcopy(near_s.at[0], near_r.at[0], 2, right)
    near1 = rcopy(near_s.at[1], near_r.at[1], 3, left)
    mrg0 = rcopy(mrg_s.at[0], mrg_r.at[0], 4, right)
    mrg1 = rcopy(mrg_s.at[1], mrg_r.at[1], 5, left)
    def far_go(h):
        far_s[half[h], :] = presum(0, h).astype(BF)
        far[h].start()

    def near0_go():
        near_s[0] = presum(1, 1).astype(BF)
        near0.start()

    def near1_go():
        near_s[1] = presum(2, 0).astype(BF)
        near1.start()

    after = {2: lambda: far_go(0), 3: lambda: far_go(1), 5: near0_go, 6: near1_go}

    def weigh_body(i, carry):
        weigh(i // 2, i % 2)
        for j in range(8):
            @pl.when(i == j)
            def _():
                sib_copy(j // 2, j % 2).start()
                if j in after:
                    after[j]()
        return carry

    lax.fori_loop(0, 8, weigh_body, 0)
    row_sums(v3, rx3, 2)
    far[0].wait_recv()
    mrg_s[0] = (presum(1, 0) + far_r[0].astype(F32)).astype(BF)
    mrg0.start()
    far[1].wait_recv()
    mrg_s[1] = (presum(2, 1) + far_r[1].astype(F32)).astype(BF)
    mrg1.start()
    acc[3, half[0], :] = presum(3, 0)
    acc[3, half[1], :] = presum(3, 1)
    from_all_dp(rx3, 2)
    t3 = jnp.sum(rx3[...], axis=0)
    row_out[...] = (EPSILON / LOG2E) * (row1 - 2.0 - jnp.log2(t3))
    roww[1] = 1.0 / t3
    spread(roww.at[1], t_b)
    near0.wait_recv()
    near1.wait_recv()
    mrg0.wait_recv()
    tgt_out[half[0], :] = ((acc[3, half[0], :] + near_r[1].astype(F32) + mrg_r[0].astype(F32)) * t_b[half[0], :]).astype(BF)
    mrg1.wait_recv()
    tgt_out[half[1], :] = ((acc[3, half[1], :] + near_r[0].astype(F32) + mrg_r[1].astype(F32)) * t_b[half[1], :]).astype(BF)

    for d in far + [near0, near1, mrg0, mrg1]:
        d.wait_send()
    for k in range(4):
        for h in range(2):
            sib_copy(k, h).wait_send()
    finish()


def place(row_in, col_in, tgt_in, row_out, col_out, tgt_out):
    row_out[...] = row_in[...]
    col_out[...] = col_in[...]
    tgt_out[...] = tgt_in[...]


def local(noise_batch, latents):
    v = pltpu.VMEM
    dma = pltpu.SemaphoreType.DMA
    row, col, tgt = pl.pallas_call(
        kernel,
        out_shape=(
            jax.ShapeDtypeStruct((8, 128), F32),
            jax.ShapeDtypeStruct((16, 128), F32),
            jax.ShapeDtypeStruct((ROWS, 128), BF),
        ),
        in_specs=[pl.BlockSpec(memory_space=pl.ANY)] * 2,
        out_specs=[pl.BlockSpec(memory_space=pltpu.VMEM)] * 3,
        scratch_shapes=[
            v((D, COLS), BF),
            v((ROWS, D), BF),
            v((ROWS, COLS), F32),
            v((ROWS, COLS), BF),
            v((D, COLS), BF),
            v((ROWS, 128), F32),
            v((ROWS, 128), F32),
            v((ROWS, 128), F32),
            v((ROWS, 128), F32),
            v((ROWS, 128), F32),
            v((16, 128), F32),
            v((2, 8, 128), F32),
            v((32, 8, 128), F32),
            v((32, 16, 128), BF),
            v((32, 16, 128), BF),
            v((32, 8, 128), F32),
            v((16, 128), F32),
            v((16, 128), F32),
            v((8, 8, 128), F32),
            v((8, 8, 128), F32),
            v((8, 8, 128), F32),
            v((4, ROWS, 128), BF),
            v((4, ROWS, 128), BF),
            v((4, ROWS, 128), F32),
            v((ROWS, 128), BF),
            v((2, ROWS // 2, 128), BF),
            v((2, ROWS // 2, 128), BF),
            v((2, ROWS // 2, 128), BF),
            v((2, ROWS // 2, 128), BF),
            v((2, ROWS // 2, 128), BF),
            dma((2,)),
            dma,
            dma((len(KEYS),)),
            dma((len(XKEYS),)),
            dma((len(XKEYS),)),
            dma((4,)),
            dma((4,)),
            dma((3,)),
            dma((3,)),
            dma((8,)),
            dma((8,)),
            dma((6,)),
            dma((6,)),
        ],
        compiler_params=pltpu.CompilerParams(
            collective_id=0, has_side_effects=True, vmem_limit_bytes=56 * 2**20),
        cost_estimate=pl.CostEstimate(flops=4 * ROWS * COLS * D, bytes_accessed=2**20, transcendentals=2 * ROWS * COLS),
    )(noise_batch, latents.T)
    row, col, tgt = pl.pallas_call(
        place,
        out_shape=(
            jax.ShapeDtypeStruct((8, 128), F32),
            jax.ShapeDtypeStruct((16, 128), F32),
            jax.ShapeDtypeStruct((ROWS, 128), BF),
        ),
        in_specs=[pl.BlockSpec(memory_space=pltpu.VMEM)] * 3,
        out_specs=[pl.BlockSpec(memory_space=pltpu.VMEM)] * 3,
        compiler_params=pltpu.CompilerParams(vmem_limit_bytes=60 * 2**20),
    )(row, col, tgt)
    return row.reshape(ROWS), col.reshape(COLS), tgt


def solution(mesh):
    in_specs = (P("noise", "dp"), P("dp", "noise"))
    out_specs = (P("noise"), P("dp"), P("noise", "dp"))
    return jax.shard_map(local, mesh=mesh, in_specs=in_specs, out_specs=out_specs, check_vma=False)
```
